512 devices in a mesh: orient: 16 (over y_hi, z), slab: 32 (over x, y_lo, core).
Axes of the slice: x: 4, y: 8 (y_hi: 2, y_lo: 4; y = y_hi * 4 + y_lo), z: 8, core: 2. Of those that a mesh axis runs over, the one named last changes fastest.
Arguments:
- images: bfloat16 [1024, 65536], P('orient', 'slab'), may hold values from -8 to 8
- projections: bfloat16 [8, 768, 65536], P(None, 'orient', 'slab'), may hold values from -0.0234375 to 0.0234375
- noise_weight: float32 [65536], P('slab'), may hold values from 0.5 to 4
- prior_score: float32 [8, 768], P(None, 'orient'), may hold values from -4 to 4
- routing: int32 [32, 768, 16, 2], P('slab', 'orient'), may hold values from 0 to 63, as said below
- insert_kernel: bfloat16 [32, 64, 128, 128], P('slab', 'orient'), may hold values from -1.5 to 1.5
Outputs:
- volume: float32 [32, 64, 8, 128], P('slab', 'orient')
The draws below stay inside these ranges and needn't reach their ends.
Inputs may be any that keep to these rules, and one draw needn't show every extreme that they name: routing[s, o, p, 0] names the slab owner that receives slice block s * 16 + p of orientation o, and routing[s, o, p, 1] a volume block of that owner's slab, below 64. Among the 768 entries with one s and one aligned block of 48 orientations, no owner is named more than 48 times, and for each aligned block of orientations there is one owner (the same for every s) that is named exactly 48 times for each s.
All inputs are finite; a program needn't handle non-finite values.
Results may differ from the reference program's by a relative error of at most 0.008.
Values may be sent and summed in bfloat16 or wider, within the bound.
No kernel may reach another device: no remote copies, remote signals or barrier semaphores. Data moves between devices by JAX's collectives and lax.ppermute only.
A program may use at most 64 MiB of HBM per device.

```python
import math
import jax
import jax.numpy as jnp
from jax import lax

K = 8
CUR = 256
PIECE = 128
ORIENT_DEV = 48
ORIENTS = 768
IMAGES = 1024
PIX = 65536
PB_DEV = 16
VB = 64
CAP = 48
N_ORIENT = 16
N_SLAB = 32


def slice_row(row_key_base, row_index):
    row_key = jax.random.fold_in(row_key_base, row_index)
    values = jnp.clip(jax.random.normal(row_key, (PIX,), jnp.float32), -6.0, 6.0)
    return values / CUR


def draw_projections(key, part):
    row_key_base = jax.random.fold_in(key, 7)
    flattened = jax.vmap(lambda row_index: slice_row(row_key_base, row_index))(jnp.arange(K * ORIENTS))
    return flattened.reshape(K, ORIENTS, PIX).astype(jnp.bfloat16)


def draw_images(key, part):
    values = jnp.clip(jax.random.normal(jax.random.fold_in(key, 31), (IMAGES, PIX), jnp.float32), -6.0, 6.0)
    return values.astype(jnp.bfloat16)


def draw_routing(key, part):
    block_size = ORIENT_DEV * PB_DEV
    spare_rows = block_size - CAP
    hot_owner = jax.random.randint(jax.random.fold_in(key, 21), (N_ORIENT,), 0, N_SLAB)
    block_key = jax.random.fold_in(key, 22)

    def one_block(slab_index, group_index):
        key_set = jax.random.split(jax.random.fold_in(jax.random.fold_in(block_key, slab_index), group_index), 3)
        position = jax.random.permutation(key_set[0], block_size).astype(jnp.int32)
        shares = jax.random.randint(key_set[1], (N_SLAB - 1,), 2, 5)
        running = jnp.cumsum(shares)
        bounds = spare_rows * running // running[-1]
        bucket = jnp.sum((position[:, None] - CAP >= bounds[None, :]).astype(jnp.int32), axis=1)
        rotation = jax.random.randint(key_set[2], (), 0, N_SLAB - 1)
        elsewhere = (hot_owner[group_index] + 1 + (bucket + rotation) % (N_SLAB - 1)) % N_SLAB
        return jnp.where(position < CAP, hot_owner[group_index], elsewhere)
    slab_ids = jnp.arange(N_SLAB)
    groups = jnp.arange(N_ORIENT)
    targets = jax.vmap(lambda slab_index: jax.vmap(lambda group_index: one_block(slab_index, group_index))(groups))(slab_ids)
    targets = targets.reshape(N_SLAB, ORIENTS, PB_DEV).astype(jnp.int32)
    voxels = jax.random.randint(jax.random.fold_in(key, 23), (N_SLAB, ORIENTS, PB_DEV), 0, VB).astype(jnp.int32)
    return jnp.stack([targets, voxels], axis=-1).astype(jnp.int32)


def shard_levels(key, dims, cuts, smallest, top_value):
    gain = 1.0
    for axis_at, parts in cuts:
        draws = jax.random.uniform(jax.random.fold_in(jax.random.fold_in(key, 6), axis_at), (parts,), jnp.float32, smallest / len(cuts), top_value / len(cuts))
        gain = gain * jnp.repeat(jnp.exp(draws), dims[axis_at] // parts).reshape((-1,) + (1,) * (len(dims) - 1 - axis_at))
    return gain


def scatter_about(stream_key, dims, scale, most, shards=(), dtype=jnp.bfloat16):
    loudness = shard_levels(stream_key, dims, shards, -0.22, 0.18) if shards else 1.0
    drawn = jax.random.normal(stream_key, dims, jnp.float32) * scale * loudness
    return jnp.minimum(jnp.maximum(drawn, -most), most).astype(dtype)


def setup_inputs(seed: int = 0) -> dict:
    streams_of = jax.random.split(jax.random.key(seed), 7)
    return {
        "images": draw_images(jax.random.fold_in(streams_of[6], 71), 0),
        "projections": draw_projections(jax.random.fold_in(streams_of[6], 71), 0),
        "noise_weight": jnp.clip(jnp.exp(math.log(4.0) - 2.0794415 * jax.random.uniform(streams_of[2], (PIX,), jnp.float32) ** shard_levels(streams_of[2], (PIX,), ((0, 32),), -0.2, 0.2)), 0.5, 4.0),
        "prior_score": scatter_about(streams_of[3], (K, ORIENTS), 1.0, 4.0, ((1, 16),), jnp.float32),
        "routing": draw_routing(jax.random.fold_in(streams_of[6], 71), 0),
        "insert_kernel": scatter_about(streams_of[5], (N_SLAB, VB, PIECE, PIECE), 16 ** -0.5, 1.5, ((0, 32), (1, 16))),
    }


def reference(images, projections, noise_weight, prior_score, routing, insert_kernel):
    def class_scores(class_slices):
        widened = class_slices.astype(jnp.float32)
        weighted = (widened * noise_weight[None, :]).astype(jnp.bfloat16)
        penalty = -0.5 * jnp.sum(widened * widened * noise_weight[None, :], axis=1)
        return jnp.dot(images, weighted.T, preferred_element_type=jnp.float32) + penalty[None, :]

    scores = lax.map(class_scores, projections) + prior_score[:, None, :]
    ceiling = jnp.max(scores, axis=(0, 2))
    total = ceiling + jnp.log(jnp.sum(jnp.exp(scores - ceiling[None, :, None]), axis=(0, 2)))
    segment_ids = (routing[..., 0] * VB + routing[..., 1]).reshape(-1)

    def class_volume(score_block):
        weights = jnp.exp(score_block - total[:, None]).astype(jnp.bfloat16)
        slices = jnp.dot(weights.T, images, preferred_element_type=jnp.float32).astype(jnp.bfloat16)
        pieces = slices.reshape(ORIENTS, N_SLAB, PB_DEV, PIECE).transpose(1, 0, 2, 3).reshape(-1, PIECE)
        return jax.ops.segment_sum(pieces.astype(jnp.float32), segment_ids, num_segments=N_SLAB * VB)

    accumulated = lax.map(class_volume, scores)
    blocks = lax.optimization_barrier(accumulated.astype(jnp.bfloat16)).astype(jnp.float32)
    blocks = blocks.reshape(K, N_SLAB, VB, PIECE)
    return jnp.einsum("ksvc,svce->svke", blocks, insert_kernel.astype(jnp.float32), precision=lax.Precision.HIGHEST)
```

```python
import jax
import jax.numpy as jnp
from jax import lax
from jax.sharding import Mesh, PartitionSpec as P

PIECE = 128
NAMES = ("yh", "z", "x", "yl", "core")
SIZES = (2, 8, 4, 4, 2)
ORIENT = ("yh", "z")
SLAB = ("x", "yl", "core")
bf16 = jnp.bfloat16
f32 = jnp.float32


def swapped(value, axis):
    return lax.ppermute(value, axis, [(0, 1), (1, 0)])


def exchanged(value, axis):
    return lax.all_to_all(value, axis, 0, 0, tiled=True)


def shared(value, axis, count):
    return exchanged(jnp.broadcast_to(value[None], (count,) + value.shape), axis)


def local(images, projections, noise_weight, prior_score, routing, insert_kernel):
    classes, orient_local, pixels = projections.shape
    columns = classes * orient_local
    rows = images.shape[0]
    orients = lax.axis_size(ORIENT)
    slabs = lax.axis_size(SLAB)
    total_rows = rows * orients
    share = total_rows // slabs
    blocks = pixels // PIECE
    pieces = orient_local * blocks
    voxels = insert_kernel.shape[1] * orients
    half = slabs // 2

    other = swapped(images, "yh")
    upper = lax.axis_index("yh") == 1
    pair = jnp.stack([jnp.where(upper, other, images), jnp.where(upper, images, other)])
    stored = lax.all_gather(pair, "z", axis=0).reshape(total_rows, pixels)

    widened = projections.astype(f32)
    product = widened * noise_weight[None, None, :]
    weighted = product.astype(bf16).reshape(columns, pixels)
    penalty = (-0.5 * jnp.sum(widened * product, axis=2)).reshape(columns)
    partial = (
        lax.dot_general(stored, weighted, (((1,), (1,)), ((), ())), preferred_element_type=f32)
        + penalty[None, :]
    )
    arrived = exchanged(partial.reshape(slabs, share, columns), SLAB)
    scores = jnp.sum(arrived, axis=0) + prior_score.reshape(columns)[None, :]
    peak = jnp.max(scores, axis=1)
    mass = jnp.sum(jnp.exp(scores - peak[:, None]), axis=1)
    stats = shared(jnp.stack([peak, mass]), ORIENT, orients)
    top = jnp.max(stats[:, 0], axis=0)
    total = top + jnp.log(jnp.sum(stats[:, 1] * jnp.exp(stats[:, 0] - top[None]), axis=0))
    own_weights = jnp.exp(scores - total[:, None]).astype(bf16)
    weights = shared(own_weights, SLAB, slabs).reshape(total_rows, classes, orient_local)
    slices = jnp.einsum(
        "iko,ipc->opkc",
        weights,
        stored.reshape(total_rows, blocks, PIECE),
        preferred_element_type=f32,
    ).astype(bf16)
    slices = slices.reshape(pieces, classes * PIECE)

    owner = routing[0, :, :, 0].reshape(pieces)
    voxel = routing[0, :, :, 1].reshape(pieces)
    far = (owner % 2) ^ lax.axis_index("core")
    slot = (far * half + owner // 2) * voxels + voxel
    placing = (
        jnp.arange(slabs * voxels, dtype=jnp.int32)[:, None] == slot[None, :]
    ).astype(bf16)
    placed = jnp.dot(placing, slices, preferred_element_type=f32)
    width = classes * PIECE
    near, away = placed[: half * voxels], placed[half * voxels :].astype(bf16)
    summed = (near + swapped(away, "core").astype(f32)).astype(bf16)
    summed = exchanged(summed.reshape(4, 4 * voxels, width), "x")
    summed = jnp.sum(summed.astype(f32), axis=0).astype(bf16)
    summed = exchanged(summed.reshape(4, voxels, width), "yl")
    summed = jnp.sum(summed.astype(f32), axis=0)
    summed = exchanged(summed.reshape(orients, voxels // orients, width), ORIENT)
    own_blocks = jnp.sum(summed, axis=0)
    rounded = own_blocks.astype(bf16).reshape(own_blocks.shape[0], classes, PIECE)
    volume = jnp.einsum("vkc,vce->vke", rounded, insert_kernel[0], preferred_element_type=f32)
    return volume[None]


def solution(mesh):
    fine = Mesh(mesh.devices.reshape(SIZES), NAMES)
    return jax.shard_map(
        local,
        mesh=fine,
        in_specs=(
            P(ORIENT, SLAB),
            P(None, ORIENT, SLAB),
            P(SLAB),
            P(None, ORIENT),
            P(SLAB, ORIENT, None, None),
            P(SLAB, ORIENT, None, None),
        ),
        out_specs=P(SLAB, ORIENT, None, None),
        check_vma=False,
    )
```

```python
import jax
import jax.numpy as jnp
from jax import lax
from jax.sharding import Mesh, PartitionSpec as P

PIECE = 128
NAMES = ("yh", "z", "x", "yl", "core")
SIZES = (2, 8, 4, 4, 2)
ORIENT = ("yh", "z")
SLAB = ("x", "yl", "core")
bf16 = jnp.bfloat16
f32 = jnp.float32


def swapped(value, axis):
    return lax.ppermute(value, axis, [(0, 1), (1, 0)])


def exchanged(value, axis):
    return lax.all_to_all(value, axis, 0, 0, tiled=True)


def shared(value, axis, count):
    return exchanged(jnp.broadcast_to(value[None], (count,) + value.shape), axis)


def turned(block, step):
    count = 8
    return lax.ppermute(block, "z", [(i, (i + step) % count) for i in range(count)])


def ring_gathered(block):
    count = 8
    z = lax.axis_index("z")
    held = jnp.zeros((count,) + block.shape, block.dtype)
    held = lax.dynamic_update_index_in_dim(held, block, z, 0)
    up = down = block
    for step in range(1, count // 2 + 1):
        up = turned(up, 1)
        held = lax.dynamic_update_index_in_dim(held, up, (z - step) % count, 0)
        if step < count // 2:
            down = turned(down, -1)
            held = lax.dynamic_update_index_in_dim(held, down, (z + step) % count, 0)
    return held


def local(images, projections, noise_weight, prior_score, routing, insert_kernel):
    classes, orient_local, pixels = projections.shape
    columns = classes * orient_local
    rows = images.shape[0]
    orients, slabs, half = 32 // 2, 32, 16
    plane_rows = rows * orients // 2
    share = plane_rows // slabs
    blocks = pixels // PIECE
    pieces = orient_local * blocks
    voxels = insert_kernel.shape[1] * orients
    core = lax.axis_index("core")
    upper = lax.axis_index("yh") == 1

    other = swapped(images, "yh")
    own_plane = ring_gathered(images).reshape(plane_rows, pixels)
    other_plane = lax.all_gather(other, "z", axis=0).reshape(plane_rows, pixels)

    widened = projections.astype(f32)
    product = widened * noise_weight[None, None, :]
    weighted = product.astype(bf16).reshape(columns, pixels)
    penalty = (-0.5 * jnp.sum(widened * product, axis=2)).reshape(columns)
    prior = prior_score.reshape(columns)

    def plane_scores(stored):
        partial = (
            lax.dot_general(stored, weighted, (((1,), (1,)), ((), ())), preferred_element_type=f32)
            + penalty[None, :]
        )
        side = plane_rows // 2
        far = lax.dynamic_slice_in_dim(partial, (1 - core) * side, side, 0)
        near = lax.dynamic_slice_in_dim(partial, core * side, side, 0)
        summed = near + swapped(far, "core")
        arrived = exchanged(summed.reshape(half, share, columns), ("x", "yl"))
        return jnp.sum(arrived, axis=0) + prior[None, :]

    scores = jnp.stack([plane_scores(own_plane), plane_scores(other_plane)])
    peak = jnp.max(scores, axis=2)
    mass = jnp.sum(jnp.exp(scores - peak[:, :, None]), axis=2)
    stats = jnp.stack([peak, mass])
    stats = jnp.where(upper, stats[:, ::-1], stats)
    stats = shared(stats.reshape(2, 2 * share), ORIENT, orients)
    top = jnp.max(stats[:, 0], axis=0)
    total = top + jnp.log(jnp.sum(stats[:, 1] * jnp.exp(stats[:, 0] - top[None]), axis=0))
    total = total.reshape(2, share)
    total = jnp.where(upper, total[::-1], total)
    own_weights = jnp.exp(scores - total[:, :, None]).astype(bf16)
    weights = shared(own_weights, ("x", "yl"), half)
    both = jnp.stack([weights, swapped(weights, "core")])
    both = jnp.where(core == 1, both[::-1], both)
    both = both.transpose(2, 0, 1, 3, 4).reshape(2, plane_rows, classes, orient_local)

    def plane_slices(plane_weights, stored):
        return jnp.einsum(
            "iko,ipc->opkc",
            plane_weights,
            stored.reshape(plane_rows, blocks, PIECE),
            preferred_element_type=f32,
        )

    slices = plane_slices(both[0], own_plane) + plane_slices(both[1], other_plane)
    slices = slices.astype(bf16).reshape(pieces, classes * PIECE)

    owner = routing[0, :, :, 0].reshape(pieces)
    voxel = routing[0, :, :, 1].reshape(pieces)
    far = (owner % 2) ^ core
    slot = (far * half + owner // 2) * voxels + voxel
    placing = (
        jnp.arange(slabs * voxels, dtype=jnp.int32)[:, None] == slot[None, :]
    ).astype(bf16)
    width = classes * PIECE
    middle = half * voxels
    away = jnp.dot(placing[middle:], slices, preferred_element_type=f32).astype(bf16)
    near = jnp.dot(placing[:middle], slices, preferred_element_type=f32)
    summed = (near + swapped(away, "core").astype(f32)).astype(bf16)
    summed = exchanged(summed.reshape(4, 4 * voxels, width), "x")
    summed = jnp.sum(summed.astype(f32), axis=0).astype(bf16)
    summed = exchanged(summed.reshape(4 * orients, voxels // orients, width), ("yl", "yh", "z"))
    own_blocks = jnp.sum(summed.astype(f32), axis=0)
    rounded = own_blocks.astype(bf16).reshape(own_blocks.shape[0], classes, PIECE)
    volume = jnp.einsum("vkc,vce->vke", rounded, insert_kernel[0], preferred_element_type=f32)
    return volume[None]


def solution(mesh):
    fine = Mesh(mesh.devices.reshape(SIZES), NAMES)
    return jax.shard_map(
        local,
        mesh=fine,
        in_specs=(
            P(ORIENT, SLAB),
            P(None, ORIENT, SLAB),
            P(SLAB),
            P(None, ORIENT),
            P(SLAB, ORIENT, None, None),
            P(SLAB, ORIENT, None, None),
        ),
        out_specs=P(SLAB, ORIENT, None, None),
        check_vma=False,
    )
```

```python
import jax
import jax.numpy as jnp
from jax import lax
from jax.experimental import pallas as pl
from jax.experimental.pallas import tpu as pltpu
from jax.sharding import Mesh, PartitionSpec as P

PIECE = 128
NAMES = ("yh", "z", "x", "yl", "core")
SIZES = (2, 8, 4, 4, 2)
ORIENT = ("yh", "z")
SLAB = ("x", "yl", "core")
bf16 = jnp.bfloat16
f32 = jnp.float32


def swapped(value, axis):
    return lax.ppermute(value, axis, [(0, 1), (1, 0)])


def exchanged(value, axis):
    return lax.all_to_all(value, axis, 0, 0, tiled=True)


def shared(value, axis, count):
    return exchanged(jnp.broadcast_to(value[None], (count,) + value.shape), axis)


def turned(block, step):
    count = 8
    return lax.ppermute(block, "z", [(i, (i + step) % count) for i in range(count)])


def ring_gathered(block):
    count = 8
    z = lax.axis_index("z")
    held = jnp.zeros((count,) + block.shape, block.dtype)
    held = lax.dynamic_update_index_in_dim(held, block, z, 0)
    up = down = block
    for step in range(1, count // 2 + 1):
        up = turned(up, 1)
        held = lax.dynamic_update_index_in_dim(held, up, (z - step) % count, 0)
        if step < count // 2:
            down = turned(down, -1)
            held = lax.dynamic_update_index_in_dim(held, down, (z + step) % count, 0)
    return held


def kernel_params():
    return pltpu.CompilerParams(vmem_limit_bytes=40 * 2**20)


def score_kernel(core_ref, image_ref, weighted_ref, penalty_ref, far_ref, near_ref):
    side = far_ref.shape[0]
    core = core_ref[0]
    for out_ref, at in ((far_ref, 1 - core), (near_ref, core)):
        rows = image_ref[pl.ds(pl.multiple_of(at * side, side), side), :]
        out_ref[...] = (
            lax.dot_general(
                rows, weighted_ref[...], (((1,), (1,)), ((), ())), preferred_element_type=f32
            )
            + penalty_ref[...]
        )


def scored(core, stored, weighted, penalty):
    rows, pixels = stored.shape
    columns = weighted.shape[0]
    side = jax.ShapeDtypeStruct((rows // 2, columns), f32)
    whole = pl.BlockSpec(memory_space=pltpu.VMEM)
    return pl.pallas_call(
        score_kernel,
        out_shape=(side, side),
        in_specs=[pl.BlockSpec(memory_space=pltpu.SMEM), whole, whole, whole],
        out_specs=(whole, whole),
        compiler_params=kernel_params(),
        cost_estimate=pl.CostEstimate(
            flops=2 * rows * pixels * columns,
            bytes_accessed=2 * pixels * (rows + columns) + 4 * rows * columns,
            transcendentals=0,
        ),
    )(core, stored, weighted, penalty)


def spots(slot_ref, start, count):
    at = start + lax.broadcasted_iota(jnp.int32, (count, slot_ref.shape[1]), 0)
    return jnp.where(at == slot_ref[...], 1.0, 0.0).astype(bf16)


def slice_kernel(
    core_ref, mine_ref, twin_ref, own_ref, other_ref, slot_ref, pieces_ref, away_ref, turned_ref
):
    step = pl.program_id(0)
    columns, rows = turned_ref.shape
    part = rows // 4
    per_class = pieces_ref.shape[0] // 16
    classes = columns // per_class

    @pl.when(step == 0)
    def _():
        for plane in range(2):
            for core in range(2):
                mine = mine_ref[:, plane].reshape(part, columns)
                twin = twin_ref[:, plane].reshape(part, columns)
                block = jnp.where(core_ref[0] == core, mine.astype(f32), twin.astype(f32))
                at = (2 * plane + core) * part
                turned_ref[:, at : at + part] = block.T.astype(bf16)

    slices = jnp.dot(
        turned_ref[:, : 2 * part], own_ref[...], preferred_element_type=f32
    ) + jnp.dot(turned_ref[:, 2 * part :], other_ref[...], preferred_element_type=f32)
    slices = slices.astype(bf16)
    many = slices.shape[1] // PIECE
    for p in range(many):
        to = pl.ds(pl.multiple_of((step * many + p) * per_class, 16), per_class)
        for k in range(classes):
            pieces_ref[to, k * PIECE : (k + 1) * PIECE] = slices[
                k * per_class : (k + 1) * per_class, p * PIECE : (p + 1) * PIECE
            ]

    @pl.when(step == pl.num_programs(0) - 1)
    def _():
        slots = away_ref.shape[0]
        for r in range(0, slots, 256):
            away_ref[r : r + 256, :] = jnp.dot(
                spots(slot_ref, slots + r, 256), pieces_ref[...], preferred_element_type=f32
            ).astype(bf16)


def sliced(core, mine, twin, own_plane, other_plane, slot, slots):
    columns = mine.shape[3]
    rows, pixels = own_plane.shape
    pieces = slot.shape[1]
    width = columns * pixels // pieces
    steps = 4
    wide = pixels // steps
    fixed = lambda rank: lambda i: (0,) * rank
    shard = pl.BlockSpec(mine.shape, fixed(4))
    band = pl.BlockSpec((rows, wide), lambda i: (0, i))
    return pl.pallas_call(
        slice_kernel,
        grid=(steps,),
        out_shape=(
            jax.ShapeDtypeStruct((pieces, width), bf16),
            jax.ShapeDtypeStruct((slots, width), bf16),
        ),
        in_specs=[
            pl.BlockSpec(memory_space=pltpu.SMEM),
            shard,
            shard,
            band,
            band,
            pl.BlockSpec(slot.shape, fixed(2)),
        ],
        out_specs=(
            pl.BlockSpec((pieces, width), fixed(2)),
            pl.BlockSpec((slots, width), fixed(2)),
        ),
        scratch_shapes=[pltpu.VMEM((columns, 2 * rows), bf16)],
        compiler_params=kernel_params(),
        cost_estimate=pl.CostEstimate(
            flops=4 * rows * pixels * columns + 2 * slots * pieces * width,
            bytes_accessed=4 * rows * pixels + 2 * width * (pieces + slots),
            transcendentals=0,
        ),
    )(core, mine, twin, own_plane, other_plane, slot)


def near_kernel(slot_ref, pieces_ref, got_ref, sum_ref):
    count = sum_ref.shape[0]
    near = jnp.dot(
        spots(slot_ref, pl.program_id(0) * count, count),
        pieces_ref[...],
        preferred_element_type=f32,
    )
    sum_ref[...] = (near + got_ref[...].astype(f32)).astype(bf16)


def near_summed(slot, pieces, got):
    slots, width = got.shape
    steps = 4
    band = pl.BlockSpec((slots // steps, width), lambda i: (i, 0))
    return pl.pallas_call(
        near_kernel,
        grid=(steps,),
        out_shape=jax.ShapeDtypeStruct(got.shape, bf16),
        in_specs=[
            pl.BlockSpec(slot.shape, lambda i: (0, 0)),
            pl.BlockSpec(pieces.shape, lambda i: (0, 0)),
            band,
        ],
        out_specs=band,
        compiler_params=kernel_params(),
        cost_estimate=pl.CostEstimate(
            flops=2 * slots * pieces.shape[0] * width,
            bytes_accessed=2 * width * (pieces.shape[0] + 2 * slots),
            transcendentals=0,
        ),
    )(slot, pieces, got)


def local(images, projections, noise_weight, prior_score, routing, insert_kernel):
    classes, orient_local, pixels = projections.shape
    columns = classes * orient_local
    rows = images.shape[0]
    orients, slabs, half = 16, 32, 16
    plane_rows = rows * orients // 2
    share = plane_rows // slabs
    blocks = pixels // PIECE
    pieces = orient_local * blocks
    voxels = insert_kernel.shape[1] * orients
    core = lax.axis_index("core")
    upper = lax.axis_index("yh") == 1
    core_one = core.reshape(1)

    where = routing[0].transpose(1, 0, 2)
    owner = where[:, :, 0].reshape(1, pieces)
    voxel = where[:, :, 1].reshape(1, pieces)
    slot = (((owner % 2) ^ core) * half + owner // 2) * voxels + voxel

    other = swapped(images, "yh")
    own_plane = lax.all_gather(images, "z", axis=0).reshape(plane_rows, pixels)
    other_plane = ring_gathered(other).reshape(plane_rows, pixels)

    widened = projections.astype(f32)
    product = widened * noise_weight[None, None, :]
    weighted = product.astype(bf16).reshape(columns, pixels)
    penalty = (-0.5 * jnp.sum(widened * product, axis=2)).reshape(1, columns)
    prior = prior_score.reshape(columns)

    def plane_scores(stored):
        far, near = scored(core_one, stored, weighted, penalty)
        return (near + swapped(far, "core")).reshape(half, share, columns)

    summed = jnp.concatenate([plane_scores(own_plane), plane_scores(other_plane)], axis=1)
    scores = jnp.sum(exchanged(summed, ("x", "yl")), axis=0) + prior[None, :]
    scores = scores.reshape(2, share, columns)
    peak = jnp.max(scores, axis=2)
    mass = jnp.sum(jnp.exp(scores - peak[:, :, None]), axis=2)
    stats = jnp.stack([peak, mass])
    stats = jnp.where(upper, stats[:, ::-1], stats)
    stats = shared(stats.reshape(2, 2 * share), ORIENT, orients)
    top = jnp.max(stats[:, 0], axis=0)
    total = top + jnp.log(jnp.sum(stats[:, 1] * jnp.exp(stats[:, 0] - top[None]), axis=0))
    total = total.reshape(2, share)
    total = jnp.where(upper, total[::-1], total)
    own_weights = jnp.exp(scores - total[:, :, None]).astype(bf16)
    mine = shared(own_weights, ("x", "yl"), half)
    twin = swapped(mine, "core")

    cut, away = sliced(core_one, mine, twin, own_plane, other_plane, slot, half * voxels)
    summed = near_summed(slot, cut, swapped(away, "core"))
    width = classes * PIECE
    summed = exchanged(summed.reshape(4, 4 * voxels, width), "x")
    summed = jnp.sum(summed.astype(f32), axis=0).astype(bf16)
    summed = exchanged(summed.reshape(4 * orients, voxels // orients, width), ("yl", "yh", "z"))
    own_blocks = jnp.sum(summed.astype(f32), axis=0)
    rounded = own_blocks.astype(bf16).reshape(own_blocks.shape[0], classes, PIECE)
    volume = jnp.einsum("vkc,vce->vke", rounded, insert_kernel[0], preferred_element_type=f32)
    return volume[None]


def solution(mesh):
    fine = Mesh(mesh.devices.reshape(SIZES), NAMES)
    return jax.shard_map(
        local,
        mesh=fine,
        in_specs=(
            P(ORIENT, SLAB),
            P(None, ORIENT, SLAB),
            P(SLAB),
            P(None, ORIENT),
            P(SLAB, ORIENT, None, None),
            P(SLAB, ORIENT, None, None),
        ),
        out_specs=P(SLAB, ORIENT, None, None),
        check_vma=False,
    )
```

```python
import functools

import jax
import jax.numpy as jnp
from jax import lax
from jax.experimental import pallas as pl
from jax.experimental.pallas import tpu as pltpu
from jax.sharding import Mesh, PartitionSpec as P

PIECE = 128
NAMES = ("yh", "z", "x", "yl", "core")
SIZES = (2, 8, 4, 4, 2)
ORIENT = ("yh", "z")
SLAB = ("x", "yl", "core")
bf16 = jnp.bfloat16
f32 = jnp.float32


def swapped(value, axis):
    return lax.ppermute(value, axis, [(0, 1), (1, 0)])


def exchanged(value, axis):
    return lax.all_to_all(value, axis, 0, 0, tiled=True)


def shared(value, axis, count):
    return exchanged(jnp.broadcast_to(value[None], (count,) + value.shape), axis)


def turned(block, step, axis="z", count=8):
    return lax.ppermute(block, axis, [(i, (i + step) % count) for i in range(count)])


def ring_gathered(block):
    count = 8
    z = lax.axis_index("z")
    held = jnp.zeros((count,) + block.shape, block.dtype)
    held = lax.dynamic_update_index_in_dim(held, block, z, 0)
    up = down = block
    for step in range(1, count // 2 + 1):
        up = turned(up, 1)
        held = lax.dynamic_update_index_in_dim(held, up, (z - step) % count, 0)
        if step < count // 2:
            down = turned(down, -1)
            held = lax.dynamic_update_index_in_dim(held, down, (z + step) % count, 0)
    return held


def kernel_params():
    return pltpu.CompilerParams(vmem_limit_bytes=24 * 2**20)


def score_kernel(core_ref, image_ref, weighted_ref, penalty_ref, far_ref, near_ref):
    side = far_ref.shape[0]
    core = core_ref[0]
    for out_ref, at in ((far_ref, 1 - core), (near_ref, core)):
        rows = image_ref[pl.ds(pl.multiple_of(at * side, side), side), :]
        out_ref[...] = (
            lax.dot_general(
                rows, weighted_ref[...], (((1,), (1,)), ((), ())), preferred_element_type=f32
            )
            + penalty_ref[...]
        )


def scored(core, stored, weighted, penalty):
    rows, pixels = stored.shape
    columns = weighted.shape[0]
    side = jax.ShapeDtypeStruct((rows // 2, columns), f32)
    whole = pl.BlockSpec(memory_space=pltpu.VMEM)
    return pl.pallas_call(
        score_kernel,
        out_shape=(side, side),
        in_specs=[pl.BlockSpec(memory_space=pltpu.SMEM), whole, whole, whole],
        out_specs=(whole, whole),
        compiler_params=kernel_params(),
        cost_estimate=pl.CostEstimate(
            flops=2 * rows * pixels * columns,
            bytes_accessed=2 * pixels * (rows + columns) + 4 * rows * columns,
            transcendentals=0,
        ),
    )(core, stored, weighted, penalty)


def spots(slot_ref, start, count):
    at = start + lax.broadcasted_iota(jnp.int32, (count, slot_ref.shape[1]), 0)
    return jnp.where(at == slot_ref[...], 1.0, 0.0).astype(bf16)


def slice_kernel(
    core_ref, mine_ref, twin_ref, other_ref, own_ref, slot_ref, pieces_ref, away_ref, turned_ref
):
    step = pl.program_id(0)
    columns, rows = turned_ref.shape
    part = rows // 4
    per_class = pieces_ref.shape[0] // 16
    classes = columns // per_class

    @pl.when(step == 0)
    def _():
        for plane in range(2):
            for core in range(2):
                mine = mine_ref[:, plane].reshape(part, columns)
                twin = twin_ref[:, plane].reshape(part, columns)
                block = jnp.where(core_ref[0] == core, mine.astype(f32), twin.astype(f32))
                at = (2 * plane + core) * part
                turned_ref[:, at : at + part] = block.T.astype(bf16)

    slices = jnp.dot(
        turned_ref[:, : 2 * part], other_ref[...], preferred_element_type=f32
    ) + jnp.dot(turned_ref[:, 2 * part :], own_ref[...], preferred_element_type=f32)
    slices = slices.astype(bf16)
    many = slices.shape[1] // PIECE
    for p in range(many):
        to = pl.ds(pl.multiple_of((step * many + p) * per_class, 16), per_class)
        for k in range(classes):
            pieces_ref[to, k * PIECE : (k + 1) * PIECE] = slices[
                k * per_class : (k + 1) * per_class, p * PIECE : (p + 1) * PIECE
            ]

    @pl.when(step == pl.num_programs(0) - 1)
    def _():
        slots = away_ref.shape[0]
        for r in range(0, slots, 256):
            away_ref[r : r + 256, :] = jnp.dot(
                spots(slot_ref, slots + r, 256), pieces_ref[...], preferred_element_type=f32
            ).astype(bf16)


def sliced(core, mine, twin, other_plane, own_plane, slot, slots):
    columns = mine.shape[3]
    rows, pixels = other_plane.shape
    pieces = slot.shape[1]
    width = columns * pixels // pieces
    steps = 4
    wide = pixels // steps
    fixed = lambda rank: lambda i: (0,) * rank
    shard = pl.BlockSpec(mine.shape, fixed(4))
    band = pl.BlockSpec((rows, wide), lambda i: (0, i))
    return pl.pallas_call(
        slice_kernel,
        grid=(steps,),
        out_shape=(
            jax.ShapeDtypeStruct((pieces, width), bf16),
            jax.ShapeDtypeStruct((slots, width), bf16),
        ),
        in_specs=[
            pl.BlockSpec(memory_space=pltpu.SMEM),
            shard,
            shard,
            band,
            band,
            pl.BlockSpec(slot.shape, fixed(2)),
        ],
        out_specs=(
            pl.BlockSpec((pieces, width), fixed(2)),
            pl.BlockSpec((slots, width), fixed(2)),
        ),
        scratch_shapes=[pltpu.VMEM((columns, 2 * rows), bf16)],
        compiler_params=kernel_params(),
        cost_estimate=pl.CostEstimate(
            flops=4 * rows * pixels * columns + 2 * slots * pieces * width,
            bytes_accessed=4 * rows * pixels + 2 * width * (pieces + slots),
            transcendentals=0,
        ),
    )(core, mine, twin, other_plane, own_plane, slot)


def near_kernel(start, slot_ref, pieces_ref, got_ref, sum_ref):
    count = sum_ref.shape[0]
    near = jnp.dot(
        spots(slot_ref, start, count), pieces_ref[...], preferred_element_type=f32
    )
    sum_ref[...] = (near + got_ref[start : start + count, :].astype(f32)).astype(sum_ref.dtype)


def near_summed(slot, pieces, got, part, dtype):
    slots, width = got.shape
    count = slots // 4
    whole = pl.BlockSpec(memory_space=pltpu.VMEM)
    return pl.pallas_call(
        functools.partial(near_kernel, part * count),
        out_shape=jax.ShapeDtypeStruct((count, width), dtype),
        in_specs=[whole] * 3,
        out_specs=whole,
        compiler_params=kernel_params(),
        cost_estimate=pl.CostEstimate(
            flops=2 * count * pieces.shape[0] * width,
            bytes_accessed=2 * width * (pieces.shape[0] + 2 * count),
            transcendentals=0,
        ),
    )(slot, pieces, got)


def local(images, projections, noise_weight, prior_score, routing, insert_kernel):
    classes, orient_local, pixels = projections.shape
    columns = classes * orient_local
    rows = images.shape[0]
    orients, slabs, half = 16, 32, 16
    plane_rows = rows * orients // 2
    share = plane_rows // slabs
    blocks = pixels // PIECE
    pieces = orient_local * blocks
    voxels = insert_kernel.shape[1] * orients
    core = lax.axis_index("core")
    upper = lax.axis_index("yh") == 0
    core_one = core.reshape(1)

    where = routing[0].transpose(1, 0, 2)
    owner = where[:, :, 0].reshape(1, pieces)
    voxel = where[:, :, 1].reshape(1, pieces)
    ahead = (owner // 8 + 4 - lax.axis_index("x")) % 4
    slot = ((((owner % 2) ^ core) * 4 + ahead) * 4 + owner // 2 % 4) * voxels + voxel

    other = swapped(images, "yh")
    other_plane = lax.all_gather(other, "z", axis=0).reshape(plane_rows, pixels)
    own_plane = ring_gathered(images).reshape(plane_rows, pixels)

    widened = projections.astype(f32)
    product = widened * noise_weight[None, None, :]
    weighted = product.astype(bf16).reshape(columns, pixels)
    penalty = (-0.5 * jnp.sum(widened * product, axis=2)).reshape(1, columns)
    prior = prior_score.reshape(columns)

    def plane_scores(stored):
        far, near = scored(core_one, stored, weighted, penalty)
        summed = (near + swapped(far, "core")).reshape(half, share, columns)
        return jnp.sum(exchanged(summed, ("x", "yl")), axis=0) + prior[None, :]

    scores = jnp.stack([plane_scores(other_plane), plane_scores(own_plane)])
    peak = jnp.max(scores, axis=2)
    mass = jnp.sum(jnp.exp(scores - peak[:, :, None]), axis=2)
    stats = jnp.stack([peak, mass])
    stats = jnp.where(upper, stats[:, ::-1], stats)
    stats = shared(stats.reshape(2, 2 * share), ORIENT, orients)
    top = jnp.max(stats[:, 0], axis=0)
    total = top + jnp.log(jnp.sum(stats[:, 1] * jnp.exp(stats[:, 0] - top[None]), axis=0))
    total = total.reshape(2, share)
    total = jnp.where(upper, total[::-1], total)
    own_weights = jnp.exp(scores - total[:, :, None]).astype(bf16)
    mine = shared(own_weights, ("x", "yl"), half)
    twin = swapped(mine, "core")

    cut, away = sliced(core_one, mine, twin, other_plane, own_plane, slot, half * voxels)
    got = swapped(away, "core")
    width = classes * PIECE
    summed = near_summed(slot, cut, got, 0, f32)
    for part in (2, 1, 3):
        sent = near_summed(slot, cut, got, part, bf16)
        summed = summed + turned(sent, part, "x", 4).astype(f32)
    summed = summed.astype(bf16)
    summed = exchanged(summed.reshape(4 * orients, voxels // orients, width), ("yl", "yh", "z"))
    own_blocks = jnp.sum(summed.astype(f32), axis=0)
    rounded = own_blocks.astype(bf16).reshape(own_blocks.shape[0], classes, PIECE)
    volume = jnp.einsum("vkc,vce->vke", rounded, insert_kernel[0], preferred_element_type=f32)
    return volume[None]


def solution(mesh):
    fine = Mesh(mesh.devices.reshape(SIZES), NAMES)
    return jax.shard_map(
        local,
        mesh=fine,
        in_specs=(
            P(ORIENT, SLAB),
            P(None, ORIENT, SLAB),
            P(SLAB),
            P(None, ORIENT),
            P(SLAB, ORIENT, None, None),
            P(SLAB, ORIENT, None, None),
        ),
        out_specs=P(SLAB, ORIENT, None, None),
        check_vma=False,
    )
```

```python
import functools

import jax
import jax.numpy as jnp
from jax import lax
from jax.experimental import pallas as pl
from jax.experimental.pallas import tpu as pltpu
from jax.sharding import Mesh, PartitionSpec as P

PIECE = 128
SCORE = 56
SLICE = 24
NAMES = ("yh", "z", "x", "yl", "core")
SIZES = (2, 8, 4, 4, 2)
ORIENT = ("yh", "z")
SLAB = ("x", "yl", "core")
bf16 = jnp.bfloat16
f32 = jnp.float32


def swapped(value, axis):
    return lax.ppermute(value, axis, [(0, 1), (1, 0)])


def exchanged(value, axis):
    return lax.all_to_all(value, axis, 0, 0, tiled=True)


def shared(value, axis, count):
    return exchanged(jnp.broadcast_to(value[None], (count,) + value.shape), axis)


def turned(block, step, axis="z", count=8):
    return lax.ppermute(block, axis, [(i, (i + step) % count) for i in range(count)])


def ring_gathered(block, later, other):
    count = 8
    z = lax.axis_index("z")
    held = jnp.zeros((count,) + block.shape, block.dtype)
    held = lax.dynamic_update_index_in_dim(held, block, z, 0)
    up, down = block, later
    for step in range(1, count // 2 + 1):
        up = turned(up, 1)
        held = lax.dynamic_update_index_in_dim(held, up, (z - step) % count, 0)
        if step < count // 2:
            if step == 2:
                down, other = lax.optimization_barrier((down, other))
            down = turned(down, -1)
            held = lax.dynamic_update_index_in_dim(held, down, (z + step) % count, 0)
    return held, other


def kernel_params(mebibytes=16):
    return pltpu.CompilerParams(vmem_limit_bytes=mebibytes * 2**20)


def score_kernel(core_ref, image_ref, weighted_ref, penalty_ref, far_ref, near_ref):
    side = far_ref.shape[0]
    core = core_ref[0]
    for out_ref, at in ((far_ref, 1 - core), (near_ref, core)):
        rows = image_ref[pl.ds(pl.multiple_of(at * side, side), side), :]
        out_ref[...] = (
            lax.dot_general(
                rows, weighted_ref[...], (((1,), (1,)), ((), ())), preferred_element_type=f32
            )
            + penalty_ref[...]
        )


def scored(core, stored, weighted, penalty):
    rows, pixels = stored.shape
    columns = weighted.shape[0]
    side = jax.ShapeDtypeStruct((rows // 2, columns), f32)
    whole = pl.BlockSpec(memory_space=pltpu.VMEM)
    return pl.pallas_call(
        score_kernel,
        out_shape=(side, side),
        in_specs=[pl.BlockSpec(memory_space=pltpu.SMEM), whole, whole, whole],
        out_specs=(whole, whole),
        compiler_params=kernel_params(SCORE),
        cost_estimate=pl.CostEstimate(
            flops=2 * rows * pixels * columns,
            bytes_accessed=2 * pixels * (rows + columns) + 4 * rows * columns,
            transcendentals=0,
        ),
    )(core, stored, weighted, penalty)


def spots(slot_ref, start, count):
    at = start + lax.broadcasted_iota(jnp.int32, (count, slot_ref.shape[1]), 0)
    return jnp.where(at == slot_ref[...], 1.0, 0.0).astype(bf16)


def slice_kernel(
    core_ref, mine_ref, twin_ref, other_ref, own_ref, slot_ref, pieces_ref, away_ref, turned_ref
):
    step = pl.program_id(0)
    columns, rows = turned_ref.shape
    part = rows // 4
    per_class = pieces_ref.shape[0] // 16
    classes = columns // per_class

    @pl.when(step == 0)
    def _():
        for plane in range(2):
            for core in range(2):
                mine = mine_ref[:, plane].reshape(part, columns)
                twin = twin_ref[:, plane].reshape(part, columns)
                block = jnp.where(core_ref[0] == core, mine.astype(f32), twin.astype(f32))
                at = (2 * plane + core) * part
                turned_ref[:, at : at + part] = block.T.astype(bf16)

    slices = jnp.dot(
        turned_ref[:, : 2 * part], other_ref[...], preferred_element_type=f32
    ) + jnp.dot(turned_ref[:, 2 * part :], own_ref[...], preferred_element_type=f32)
    slices = slices.astype(bf16)
    many = slices.shape[1] // PIECE
    for p in range(many):
        to = pl.ds(pl.multiple_of((step * many + p) * per_class, 16), per_class)
        for k in range(classes):
            pieces_ref[to, k * PIECE : (k + 1) * PIECE] = slices[
                k * per_class : (k + 1) * per_class, p * PIECE : (p + 1) * PIECE
            ]

    @pl.when(step == pl.num_programs(0) - 1)
    def _():
        count = away_ref.shape[0]
        away_ref[...] = jnp.dot(
            spots(slot_ref, 6 * count, count), pieces_ref[...], preferred_element_type=f32
        ).astype(bf16)


def sliced(core, mine, twin, other_plane, own_plane, slot, slots):
    columns = mine.shape[3]
    rows, pixels = other_plane.shape
    pieces = slot.shape[1]
    width = columns * pixels // pieces
    steps = 4
    wide = pixels // steps
    fixed = lambda rank: lambda i: (0,) * rank
    shard = pl.BlockSpec(mine.shape, fixed(4))
    band = pl.BlockSpec((rows, wide), lambda i: (0, i))
    return pl.pallas_call(
        slice_kernel,
        grid=(steps,),
        out_shape=(
            jax.ShapeDtypeStruct((pieces, width), bf16),
            jax.ShapeDtypeStruct((slots, width), bf16),
        ),
        in_specs=[
            pl.BlockSpec(memory_space=pltpu.SMEM),
            shard,
            shard,
            band,
            band,
            pl.BlockSpec(slot.shape, fixed(2)),
        ],
        out_specs=(
            pl.BlockSpec((pieces, width), fixed(2)),
            pl.BlockSpec((slots, width), fixed(2)),
        ),
        scratch_shapes=[pltpu.VMEM((columns, 2 * rows), bf16)],
        compiler_params=kernel_params(SLICE),
        cost_estimate=pl.CostEstimate(
            flops=4 * rows * pixels * columns + 2 * slots * pieces * width,
            bytes_accessed=4 * rows * pixels + 2 * width * (pieces + slots),
            transcendentals=0,
        ),
    )(core, mine, twin, other_plane, own_plane, slot)


def away_kernel(slot_ref, pieces_ref, away_ref):
    count = away_ref.shape[0] // 3
    for row, part in enumerate((1, 3, 0)):
        away_ref[row * count : (row + 1) * count, :] = jnp.dot(
            spots(slot_ref, (4 + part) * count, count),
            pieces_ref[...],
            preferred_element_type=f32,
        ).astype(bf16)


def near_kernel(part, row, lead, slot_ref, pieces_ref, got_ref, *refs):
    count = refs[-1].shape[0]
    near = jnp.dot(
        spots(slot_ref, part * count, count), pieces_ref[...], preferred_element_type=f32
    ) + got_ref[row * count : (row + 1) * count, :].astype(f32)
    if part == 2:
        half = near.shape[1] // 2
        refs[0][...] = near[:, :half].astype(bf16)
        refs[1][...] = near[:, half:].astype(bf16)
    elif part == 0:
        refs[0][...] = near
    else:
        passed_ref, sum_ref = refs
        half = passed_ref.shape[1]
        added = slice(lead, lead + half)
        other = slice(half - lead, 2 * half - lead)
        sum_ref[:, added] = (near[:, added] + passed_ref[...].astype(f32)).astype(bf16)
        sum_ref[:, other] = near[:, other].astype(bf16)


def whole_call(kernel, outs, flops, *args):
    whole = pl.BlockSpec(memory_space=pltpu.VMEM)
    moved = sum(x.size * x.dtype.itemsize for x in args)
    return pl.pallas_call(
        kernel,
        out_shape=outs,
        in_specs=[whole] * len(args),
        out_specs=jax.tree.map(lambda _: whole, outs),
        compiler_params=kernel_params(),
        cost_estimate=pl.CostEstimate(flops=flops, bytes_accessed=moved, transcendentals=0),
    )(*args)


def slots_summed(slot, cut, away, count):
    pieces, width = cut.shape
    flops = 2 * count * pieces * width
    shape = lambda wide, dtype: jax.ShapeDtypeStruct((count, wide), dtype)
    far = swapped(away, "core")
    rest = jax.ShapeDtypeStruct((3 * count, width), bf16)
    rest = swapped(whole_call(away_kernel, rest, 3 * flops, slot, cut), "core")

    def near(part, row, lead, outs, *args):
        kernel = functools.partial(near_kernel, part, row, lead)
        return whole_call(kernel, outs, flops, slot, cut, *args)

    halves = (shape(width // 2, bf16),) * 2
    left, right = near(2, 0, 0, halves, far)
    left, right = turned(left, 1, "x", 4), turned(right, -1, "x", 4)
    summed = near(0, 2, 0, shape(width, f32), rest)
    one = turned(near(1, 0, 0, shape(width, bf16), rest, left), 1, "x", 4)
    three = turned(near(3, 1, width // 2, shape(width, bf16), rest, right), -1, "x", 4)
    return (summed + one.astype(f32) + three.astype(f32)).astype(bf16)


def local(images, projections, noise_weight, prior_score, routing, insert_kernel):
    classes, orient_local, pixels = projections.shape
    columns = classes * orient_local
    rows = images.shape[0]
    orients, slabs, half = 16, 32, 16
    plane_rows = rows * orients // 2
    share = plane_rows // slabs
    blocks = pixels // PIECE
    pieces = orient_local * blocks
    voxels = insert_kernel.shape[1] * orients
    core = lax.axis_index("core")
    upper = lax.axis_index("yh") == 0
    core_one = core.reshape(1)

    where = routing[0].transpose(1, 0, 2)
    owner = where[:, :, 0].reshape(1, pieces)
    voxel = where[:, :, 1].reshape(1, pieces)
    ahead = (owner // 8 + 4 - lax.axis_index("x")) % 4
    slot = ((((owner % 2) ^ core) * 4 + ahead) * 4 + owner // 2 % 4) * voxels + voxel

    other = swapped(images, "yh")

    widened = projections.astype(f32)
    product = widened * noise_weight[None, None, :]
    weighted = product.astype(bf16).reshape(columns, pixels)
    penalty = (-0.5 * jnp.sum(widened * product, axis=2)).reshape(1, columns)
    prior = prior_score.reshape(columns)
    later, penalty = lax.optimization_barrier((images, penalty))
    own_plane, other = ring_gathered(images, later, other)
    own_plane = own_plane.reshape(plane_rows, pixels)
    other_plane = lax.all_gather(other, "z", axis=0).reshape(plane_rows, pixels)

    def plane_scores(stored):
        far, near = scored(core_one, stored, weighted, penalty)
        summed = (near + swapped(far, "core")).reshape(half, share, columns)
        return jnp.sum(exchanged(summed, ("x", "yl")), axis=0) + prior[None, :]

    scores = jnp.stack([plane_scores(other_plane), plane_scores(own_plane)])
    peak = jnp.max(scores, axis=2)
    mass = jnp.sum(jnp.exp(scores - peak[:, :, None]), axis=2)
    stats = jnp.stack([peak, mass])
    stats = jnp.where(upper, stats[:, ::-1], stats)
    stats = shared(stats.reshape(2, 2 * share), ORIENT, orients)
    top = jnp.max(stats[:, 0], axis=0)
    total = top + jnp.log(jnp.sum(stats[:, 1] * jnp.exp(stats[:, 0] - top[None]), axis=0))
    total = total.reshape(2, share)
    total = jnp.where(upper, total[::-1], total)
    own_weights = jnp.exp(scores - total[:, :, None]).astype(bf16)
    mine = shared(own_weights, ("x", "yl"), half)
    twin = swapped(mine, "core")

    cut, away = sliced(core_one, mine, twin, other_plane, own_plane, slot, 4 * voxels)
    width = classes * PIECE
    summed = slots_summed(slot, cut, away, 4 * voxels)
    summed = exchanged(summed.reshape(4 * orients, voxels // orients, width), ("yl", "yh", "z"))
    own_blocks = jnp.sum(summed.astype(f32), axis=0)
    rounded = own_blocks.astype(bf16).reshape(own_blocks.shape[0], classes, PIECE)
    volume = jnp.einsum("vkc,vce->vke", rounded, insert_kernel[0], preferred_element_type=f32)
    return volume[None]


def solution(mesh):
    fine = Mesh(mesh.devices.reshape(SIZES), NAMES)
    return jax.shard_map(
        local,
        mesh=fine,
        in_specs=(
            P(ORIENT, SLAB),
            P(None, ORIENT, SLAB),
            P(SLAB),
            P(None, ORIENT),
            P(SLAB, ORIENT, None, None),
            P(SLAB, ORIENT, None, None),
        ),
        out_specs=P(SLAB, ORIENT, None, None),
        check_vma=False,
    )
```

```python
import functools

import jax
import jax.numpy as jnp
from jax import lax
from jax.experimental import pallas as pl
from jax.experimental.pallas import tpu as pltpu
from jax.sharding import Mesh, PartitionSpec as P

PIECE = 128
NAMES = ("yh", "z", "x", "yl", "core")
SIZES = (2, 8, 4, 4, 2)
ORIENT = ("yh", "z")
SLAB = ("x", "yl", "core")
bf16 = jnp.bfloat16
f32 = jnp.float32


def swapped(value, axis):
    return lax.ppermute(value, axis, [(0, 1), (1, 0)])


def exchanged(value, axis):
    return lax.all_to_all(value, axis, 0, 0, tiled=True)


def shared(value, axis, count):
    return exchanged(jnp.broadcast_to(value[None], (count,) + value.shape), axis)


def turned(block, step, axis="z", count=8):
    return lax.ppermute(block, axis, [(i, (i + step) % count) for i in range(count)])


STEPS = (0, 1, -1, 2, -2, 3, -3, 4)


def ring_gathered(block, held_back):
    got = [block]
    up = down = block
    for step in range(1, 5):
        if step == 2:
            up, held_back = lax.optimization_barrier((up, held_back))
        up = turned(up, 1)
        got.append(up)
        if step < 4:
            down = turned(down, -1)
            got.append(down)
    return got, held_back


def kernel_params():
    return pltpu.CompilerParams(vmem_limit_bytes=24 * 2**20)


def ring_score_kernel(core_ref, z_ref, *refs):
    blocks, (weighted_ref, penalty_ref, far_ref, near_ref, plane_ref) = refs[:-5], refs[-5:]
    rows = blocks[0].shape[0]
    for step, block_ref in zip(STEPS, blocks):
        owner = lax.rem(z_ref[0] + 8 - step, 8)
        plane_ref[pl.ds(pl.multiple_of(owner * rows, rows), rows), :] = block_ref[...]
    score_kernel(core_ref, plane_ref, weighted_ref, penalty_ref, far_ref, near_ref)


def ring_scored(core, z, blocks, weighted, penalty):
    rows, pixels = blocks[0].shape
    rows *= len(blocks)
    columns = weighted.shape[0]
    side = jax.ShapeDtypeStruct((rows // 2, columns), f32)
    whole = pl.BlockSpec(memory_space=pltpu.VMEM)
    one = pl.BlockSpec(memory_space=pltpu.SMEM)
    return pl.pallas_call(
        ring_score_kernel,
        out_shape=(side, side, jax.ShapeDtypeStruct((rows, pixels), bf16)),
        in_specs=[one, one] + [whole] * (len(blocks) + 2),
        out_specs=(whole, whole, whole),
        compiler_params=kernel_params(),
        cost_estimate=pl.CostEstimate(
            flops=2 * rows * pixels * columns,
            bytes_accessed=2 * pixels * (2 * rows + columns) + 4 * rows * columns,
            transcendentals=0,
        ),
    )(core, z, *blocks, weighted, penalty)


def score_kernel(core_ref, image_ref, weighted_ref, penalty_ref, far_ref, near_ref):
    side = far_ref.shape[0]
    core = core_ref[0]
    for out_ref, at in ((far_ref, 1 - core), (near_ref, core)):
        rows = image_ref[pl.ds(pl.multiple_of(at * side, side), side), :]
        out_ref[...] = (
            lax.dot_general(
                rows, weighted_ref[...], (((1,), (1,)), ((), ())), preferred_element_type=f32
            )
            + penalty_ref[...]
        )


def scored(core, stored, weighted, penalty):
    rows, pixels = stored.shape
    columns = weighted.shape[0]
    side = jax.ShapeDtypeStruct((rows // 2, columns), f32)
    whole = pl.BlockSpec(memory_space=pltpu.VMEM)
    return pl.pallas_call(
        score_kernel,
        out_shape=(side, side),
        in_specs=[pl.BlockSpec(memory_space=pltpu.SMEM), whole, whole, whole],
        out_specs=(whole, whole),
        compiler_params=kernel_params(),
        cost_estimate=pl.CostEstimate(
            flops=2 * rows * pixels * columns,
            bytes_accessed=2 * pixels * (rows + columns) + 4 * rows * columns,
            transcendentals=0,
        ),
    )(core, stored, weighted, penalty)


def spots(slot_ref, start, count):
    at = start + lax.broadcasted_iota(jnp.int32, (count, slot_ref.shape[1]), 0)
    return jnp.where(at == slot_ref[...], 1.0, 0.0).astype(bf16)


def slice_kernel(
    core_ref, mine_ref, twin_ref, other_ref, own_ref, slot_ref, pieces_ref, away_ref, turned_ref
):
    step = pl.program_id(0)
    columns, rows = turned_ref.shape
    part = rows // 4
    per_class = pieces_ref.shape[0] // 16
    classes = columns // per_class

    @pl.when(step == 0)
    def _():
        for plane in range(2):
            for core in range(2):
                mine = mine_ref[:, plane].reshape(part, columns)
                twin = twin_ref[:, plane].reshape(part, columns)
                block = jnp.where(core_ref[0] == core, mine.astype(f32), twin.astype(f32))
                at = (2 * plane + core) * part
                turned_ref[:, at : at + part] = block.T.astype(bf16)

    slices = jnp.dot(
        turned_ref[:, : 2 * part], other_ref[...], preferred_element_type=f32
    ) + jnp.dot(turned_ref[:, 2 * part :], own_ref[...], preferred_element_type=f32)
    slices = slices.astype(bf16)
    many = slices.shape[1] // PIECE
    for p in range(many):
        to = pl.ds(pl.multiple_of((step * many + p) * per_class, 16), per_class)
        for k in range(classes):
            pieces_ref[to, k * PIECE : (k + 1) * PIECE] = slices[
                k * per_class : (k + 1) * per_class, p * PIECE : (p + 1) * PIECE
            ]

    @pl.when(step == pl.num_programs(0) - 1)
    def _():
        slots = away_ref.shape[0]
        for r in range(0, slots, 256):
            away_ref[r : r + 256, :] = jnp.dot(
                spots(slot_ref, slots + r, 256), pieces_ref[...], preferred_element_type=f32
            ).astype(bf16)


def sliced(core, mine, twin, other_plane, own_plane, slot, slots):
    columns = mine.shape[3]
    rows, pixels = other_plane.shape
    pieces = slot.shape[1]
    width = columns * pixels // pieces
    steps = 4
    wide = pixels // steps
    fixed = lambda rank: lambda i: (0,) * rank
    shard = pl.BlockSpec(mine.shape, fixed(4))
    band = pl.BlockSpec((rows, wide), lambda i: (0, i))
    return pl.pallas_call(
        slice_kernel,
        grid=(steps,),
        out_shape=(
            jax.ShapeDtypeStruct((pieces, width), bf16),
            jax.ShapeDtypeStruct((slots, width), bf16),
        ),
        in_specs=[
            pl.BlockSpec(memory_space=pltpu.SMEM),
            shard,
            shard,
            band,
            band,
            pl.BlockSpec(slot.shape, fixed(2)),
        ],
        out_specs=(
            pl.BlockSpec((pieces, width), fixed(2)),
            pl.BlockSpec((slots, width), fixed(2)),
        ),
        scratch_shapes=[pltpu.VMEM((columns, 2 * rows), bf16)],
        compiler_params=kernel_params(),
        cost_estimate=pl.CostEstimate(
            flops=4 * rows * pixels * columns + 2 * slots * pieces * width,
            bytes_accessed=4 * rows * pixels + 2 * width * (pieces + slots),
            transcendentals=0,
        ),
    )(core, mine, twin, other_plane, own_plane, slot)


def near_kernel(start, slot_ref, pieces_ref, got_ref, sum_ref):
    count = sum_ref.shape[0]
    near = jnp.dot(
        spots(slot_ref, start, count), pieces_ref[...], preferred_element_type=f32
    )
    sum_ref[...] = (near + got_ref[start : start + count, :].astype(f32)).astype(sum_ref.dtype)


def near_summed(slot, pieces, got, part, dtype):
    slots, width = got.shape
    count = slots // 4
    whole = pl.BlockSpec(memory_space=pltpu.VMEM)
    return pl.pallas_call(
        functools.partial(near_kernel, part * count),
        out_shape=jax.ShapeDtypeStruct((count, width), dtype),
        in_specs=[whole] * 3,
        out_specs=whole,
        compiler_params=kernel_params(),
        cost_estimate=pl.CostEstimate(
            flops=2 * count * pieces.shape[0] * width,
            bytes_accessed=2 * width * (pieces.shape[0] + 2 * count),
            transcendentals=0,
        ),
    )(slot, pieces, got)


def local(images, projections, noise_weight, prior_score, routing, insert_kernel):
    classes, orient_local, pixels = projections.shape
    columns = classes * orient_local
    rows = images.shape[0]
    orients, slabs, half = 16, 32, 16
    plane_rows = rows * orients // 2
    share = plane_rows // slabs
    blocks = pixels // PIECE
    pieces = orient_local * blocks
    voxels = insert_kernel.shape[1] * orients
    core = lax.axis_index("core")
    upper = lax.axis_index("yh") == 0
    core_one = core.reshape(1)

    where = routing[0].transpose(1, 0, 2)
    owner = where[:, :, 0].reshape(1, pieces)
    voxel = where[:, :, 1].reshape(1, pieces)
    ahead = (owner // 8 + 4 - lax.axis_index("x")) % 4
    slot = ((((owner % 2) ^ core) * 4 + ahead) * 4 + owner // 2 % 4) * voxels + voxel

    other = swapped(images, "yh")
    ring, other = ring_gathered(images, other)
    other_plane = lax.all_gather(other, "z", axis=0).reshape(plane_rows, pixels)

    widened = projections.astype(f32)
    product = widened * noise_weight[None, None, :]
    weighted = product.astype(bf16).reshape(columns, pixels)
    penalty = (-0.5 * jnp.sum(widened * product, axis=2)).reshape(1, columns)
    prior = prior_score.reshape(columns)

    def summed_scores(far, near):
        summed = (near + swapped(far, "core")).reshape(half, share, columns)
        return jnp.sum(exchanged(summed, ("x", "yl")), axis=0) + prior[None, :]

    z_one = lax.axis_index("z").reshape(1)
    far, near, own_plane = ring_scored(core_one, z_one, ring, weighted, penalty)
    own_scores = summed_scores(far, near)
    other_scores = summed_scores(*scored(core_one, other_plane, weighted, penalty))
    scores = jnp.stack([other_scores, own_scores])
    peak = jnp.max(scores, axis=2)
    mass = jnp.sum(jnp.exp(scores - peak[:, :, None]), axis=2)
    stats = jnp.stack([peak, mass])
    stats = jnp.where(upper, stats[:, ::-1], stats)
    stats = shared(stats.reshape(2, 2 * share), ORIENT, orients)
    top = jnp.max(stats[:, 0], axis=0)
    total = top + jnp.log(jnp.sum(stats[:, 1] * jnp.exp(stats[:, 0] - top[None]), axis=0))
    total = total.reshape(2, share)
    total = jnp.where(upper, total[::-1], total)
    own_weights = jnp.exp(scores - total[:, :, None]).astype(bf16)
    mine = shared(own_weights, ("x", "yl"), half)
    twin = swapped(mine, "core")

    cut, away = sliced(core_one, mine, twin, other_plane, own_plane, slot, half * voxels)
    got = swapped(away, "core")
    width = classes * PIECE
    summed = near_summed(slot, cut, got, 0, f32)
    for part in (2, 1, 3):
        sent = near_summed(slot, cut, got, part, bf16)
        summed = summed + turned(sent, part, "x", 4).astype(f32)
    summed = summed.astype(bf16)
    summed = exchanged(summed.reshape(4 * orients, voxels // orients, width), ("yl", "yh", "z"))
    own_blocks = jnp.sum(summed.astype(f32), axis=0)
    rounded = own_blocks.astype(bf16).reshape(own_blocks.shape[0], classes, PIECE)
    volume = jnp.einsum("vkc,vce->vke", rounded, insert_kernel[0], preferred_element_type=f32)
    return volume[None]


def solution(mesh):
    fine = Mesh(mesh.devices.reshape(SIZES), NAMES)
    return jax.shard_map(
        local,
        mesh=fine,
        in_specs=(
            P(ORIENT, SLAB),
            P(None, ORIENT, SLAB),
            P(SLAB),
            P(None, ORIENT),
            P(SLAB, ORIENT, None, None),
            P(SLAB, ORIENT, None, None),
        ),
        out_specs=P(SLAB, ORIENT, None, None),
        check_vma=False,
    )
```

```python
import functools

import jax
import jax.numpy as jnp
from jax import lax
from jax.experimental import pallas as pl
from jax.experimental.pallas import tpu as pltpu
from jax.sharding import Mesh, PartitionSpec as P

PIECE = 128
NAMES = ("yh", "z", "x", "yl", "core")
SIZES = (2, 8, 4, 4, 2)
ORIENT = ("yh", "z")
SLAB = ("x", "yl", "core")
bf16 = jnp.bfloat16
f32 = jnp.float32


def swapped(value, axis):
    return lax.ppermute(value, axis, [(0, 1), (1, 0)])


def exchanged(value, axis):
    return lax.all_to_all(value, axis, 0, 0, tiled=True)


def shared(value, axis, count):
    return exchanged(jnp.broadcast_to(value[None], (count,) + value.shape), axis)


def turned(block, step, axis="z", count=8):
    return lax.ppermute(block, axis, [(i, (i + step) % count) for i in range(count)])


STEPS = (0, 1, -1, 2, -2, 3, -3, 4)


def ring_gathered(block, held_back):
    got = [block]
    up = down = block
    for step in range(1, 5):
        up = turned(up, 1)
        got.append(up)
        if step < 4:
            down = turned(down, -1)
            got.append(down)
        if step == 2:
            held_back = lax.optimization_barrier((up, down, held_back))[2]
    return got, held_back


def kernel_params():
    return pltpu.CompilerParams(vmem_limit_bytes=24 * 2**20)


def ring_score_kernel(core_ref, z_ref, *refs):
    blocks, (weighted_ref, penalty_ref, far_ref, near_ref, plane_ref) = refs[:-5], refs[-5:]
    rows = blocks[0].shape[0]
    for step, block_ref in zip(STEPS, blocks):
        owner = lax.rem(z_ref[0] + 8 - step, 8)
        plane_ref[pl.ds(pl.multiple_of(owner * rows, rows), rows), :] = block_ref[...]
    score_kernel(core_ref, plane_ref, weighted_ref, penalty_ref, far_ref, near_ref)


def ring_scored(core, z, blocks, weighted, penalty):
    rows, pixels = blocks[0].shape
    rows *= len(blocks)
    columns = weighted.shape[0]
    side = jax.ShapeDtypeStruct((rows // 2, columns), f32)
    whole = pl.BlockSpec(memory_space=pltpu.VMEM)
    one = pl.BlockSpec(memory_space=pltpu.SMEM)
    return pl.pallas_call(
        ring_score_kernel,
        out_shape=(side, side, jax.ShapeDtypeStruct((rows, pixels), bf16)),
        in_specs=[one, one] + [whole] * (len(blocks) + 2),
        out_specs=(whole, whole, whole),
        compiler_params=kernel_params(),
        cost_estimate=pl.CostEstimate(
            flops=2 * rows * pixels * columns,
            bytes_accessed=2 * pixels * (2 * rows + columns) + 4 * rows * columns,
            transcendentals=0,
        ),
    )(core, z, *blocks, weighted, penalty)


def score_kernel(core_ref, image_ref, weighted_ref, penalty_ref, far_ref, near_ref):
    side = far_ref.shape[0]
    core = core_ref[0]
    for out_ref, at in ((far_ref, 1 - core), (near_ref, core)):
        rows = image_ref[pl.ds(pl.multiple_of(at * side, side), side), :]
        out_ref[...] = (
            lax.dot_general(
                rows, weighted_ref[...], (((1,), (1,)), ((), ())), preferred_element_type=f32
            )
            + penalty_ref[...]
        )


def scored(core, stored, weighted, penalty):
    rows, pixels = stored.shape
    columns = weighted.shape[0]
    side = jax.ShapeDtypeStruct((rows // 2, columns), f32)
    whole = pl.BlockSpec(memory_space=pltpu.VMEM)
    return pl.pallas_call(
        score_kernel,
        out_shape=(side, side),
        in_specs=[pl.BlockSpec(memory_space=pltpu.SMEM), whole, whole, whole],
        out_specs=(whole, whole),
        compiler_params=kernel_params(),
        cost_estimate=pl.CostEstimate(
            flops=2 * rows * pixels * columns,
            bytes_accessed=2 * pixels * (rows + columns) + 4 * rows * columns,
            transcendentals=0,
        ),
    )(core, stored, weighted, penalty)


def spots(slot_ref, start, count):
    at = start + lax.broadcasted_iota(jnp.int32, (count, slot_ref.shape[1]), 0)
    return jnp.where(at == slot_ref[...], 1.0, 0.0).astype(bf16)


def slice_kernel(
    core_ref, mine_ref, twin_ref, other_ref, own_ref, slot_ref, pieces_ref, away_ref, turned_ref
):
    step = pl.program_id(0)
    columns, rows = turned_ref.shape
    part = rows // 4
    per_class = pieces_ref.shape[0] // 16
    classes = columns // per_class

    @pl.when(step == 0)
    def _():
        for plane in range(2):
            for core in range(2):
                mine = mine_ref[:, plane].reshape(part, columns)
                twin = twin_ref[:, plane].reshape(part, columns)
                block = jnp.where(core_ref[0] == core, mine.astype(f32), twin.astype(f32))
                at = (2 * plane + core) * part
                turned_ref[:, at : at + part] = block.T.astype(bf16)

    slices = jnp.dot(
        turned_ref[:, : 2 * part], other_ref[...], preferred_element_type=f32
    ) + jnp.dot(turned_ref[:, 2 * part :], own_ref[...], preferred_element_type=f32)
    slices = slices.astype(bf16)
    many = slices.shape[1] // PIECE
    for p in range(many):
        to = pl.ds(pl.multiple_of((step * many + p) * per_class, 16), per_class)
        for k in range(classes):
            pieces_ref[to, k * PIECE : (k + 1) * PIECE] = slices[
                k * per_class : (k + 1) * per_class, p * PIECE : (p + 1) * PIECE
            ]

    @pl.when(step == pl.num_programs(0) - 1)
    def _():
        slots = away_ref.shape[0]
        for r in range(0, slots, 256):
            away_ref[r : r + 256, :] = jnp.dot(
                spots(slot_ref, slots + r, 256), pieces_ref[...], preferred_element_type=f32
            ).astype(bf16)


def sliced(core, mine, twin, other_plane, own_plane, slot, slots):
    columns = mine.shape[3]
    rows, pixels = other_plane.shape
    pieces = slot.shape[1]
    width = columns * pixels // pieces
    steps = 4
    wide = pixels // steps
    fixed = lambda rank: lambda i: (0,) * rank
    shard = pl.BlockSpec(mine.shape, fixed(4))
    band = pl.BlockSpec((rows, wide), lambda i: (0, i))
    return pl.pallas_call(
        slice_kernel,
        grid=(steps,),
        out_shape=(
            jax.ShapeDtypeStruct((pieces, width), bf16),
            jax.ShapeDtypeStruct((slots, width), bf16),
        ),
        in_specs=[
            pl.BlockSpec(memory_space=pltpu.SMEM),
            shard,
            shard,
            band,
            band,
            pl.BlockSpec(slot.shape, fixed(2)),
        ],
        out_specs=(
            pl.BlockSpec((pieces, width), fixed(2)),
            pl.BlockSpec((slots, width), fixed(2)),
        ),
        scratch_shapes=[pltpu.VMEM((columns, 2 * rows), bf16)],
        compiler_params=kernel_params(),
        cost_estimate=pl.CostEstimate(
            flops=4 * rows * pixels * columns + 2 * slots * pieces * width,
            bytes_accessed=4 * rows * pixels + 2 * width * (pieces + slots),
            transcendentals=0,
        ),
    )(core, mine, twin, other_plane, own_plane, slot)


def near_kernel(start, slot_ref, pieces_ref, got_ref, sum_ref):
    count = sum_ref.shape[0]
    near = jnp.dot(
        spots(slot_ref, start, count), pieces_ref[...], preferred_element_type=f32
    )
    sum_ref[...] = (near + got_ref[start : start + count, :].astype(f32)).astype(sum_ref.dtype)


def near_summed(slot, pieces, got, part, dtype):
    slots, width = got.shape
    count = slots // 4
    whole = pl.BlockSpec(memory_space=pltpu.VMEM)
    return pl.pallas_call(
        functools.partial(near_kernel, part * count),
        out_shape=jax.ShapeDtypeStruct((count, width), dtype),
        in_specs=[whole] * 3,
        out_specs=whole,
        compiler_params=kernel_params(),
        cost_estimate=pl.CostEstimate(
            flops=2 * count * pieces.shape[0] * width,
            bytes_accessed=2 * width * (pieces.shape[0] + 2 * count),
            transcendentals=0,
        ),
    )(slot, pieces, got)


def local(images, projections, noise_weight, prior_score, routing, insert_kernel):
    classes, orient_local, pixels = projections.shape
    columns = classes * orient_local
    rows = images.shape[0]
    orients, slabs, half = 16, 32, 16
    plane_rows = rows * orients // 2
    share = plane_rows // slabs
    blocks = pixels // PIECE
    pieces = orient_local * blocks
    voxels = insert_kernel.shape[1] * orients
    core = lax.axis_index("core")
    upper = lax.axis_index("yh") == 0
    core_one = core.reshape(1)

    where = routing[0].transpose(1, 0, 2)
    owner = where[:, :, 0].reshape(1, pieces)
    voxel = where[:, :, 1].reshape(1, pieces)
    ahead = (owner // 8 + 4 - lax.axis_index("x")) % 4
    slot = ((((owner % 2) ^ core) * 4 + ahead) * 4 + owner // 2 % 4) * voxels + voxel

    other = swapped(images, "yh")
    ring, other = ring_gathered(images, other)
    other_plane = lax.all_gather(other, "z", axis=0).reshape(plane_rows, pixels)

    widened = projections.astype(f32)
    product = widened * noise_weight[None, None, :]
    weighted = product.astype(bf16).reshape(columns, pixels)
    penalty = (-0.5 * jnp.sum(widened * product, axis=2)).reshape(1, columns)
    prior = prior_score.reshape(columns)

    def summed_scores(far, near):
        summed = (near + swapped(far, "core")).reshape(half, share, columns)
        return jnp.sum(exchanged(summed, ("x", "yl")), axis=0) + prior[None, :]

    z_one = lax.axis_index("z").reshape(1)
    far, near, own_plane = ring_scored(core_one, z_one, ring, weighted, penalty)
    own_scores = summed_scores(far, near)
    other_scores = summed_scores(*scored(core_one, other_plane, weighted, penalty))
    scores = jnp.stack([other_scores, own_scores])
    peak = jnp.max(scores, axis=2)
    mass = jnp.sum(jnp.exp(scores - peak[:, :, None]), axis=2)
    stats = jnp.stack([peak, mass])
    stats = jnp.where(upper, stats[:, ::-1], stats)
    stats = shared(stats.reshape(2, 2 * share), ORIENT, orients)
    top = jnp.max(stats[:, 0], axis=0)
    total = top + jnp.log(jnp.sum(stats[:, 1] * jnp.exp(stats[:, 0] - top[None]), axis=0))
    total = total.reshape(2, share)
    total = jnp.where(upper, total[::-1], total)
    own_weights = jnp.exp(scores - total[:, :, None]).astype(bf16)
    mine = shared(own_weights, ("x", "yl"), half)
    twin = swapped(mine, "core")

    cut, away = sliced(core_one, mine, twin, other_plane, own_plane, slot, half * voxels)
    got = swapped(away, "core")
    width = classes * PIECE
    summed = near_summed(slot, cut, got, 0, f32)
    for part in (2, 1, 3):
        sent = near_summed(slot, cut, got, part, bf16)
        summed = summed + turned(sent, part, "x", 4).astype(f32)
    summed = summed.astype(bf16)
    summed = exchanged(summed.reshape(4 * orients, voxels // orients, width), ("yl", "yh", "z"))
    own_blocks = jnp.sum(summed.astype(f32), axis=0)
    rounded = own_blocks.astype(bf16).reshape(own_blocks.shape[0], classes, PIECE)
    volume = jnp.einsum("vkc,vce->vke", rounded, insert_kernel[0], preferred_element_type=f32)
    return volume[None]


def solution(mesh):
    fine = Mesh(mesh.devices.reshape(SIZES), NAMES)
    return jax.shard_map(
        local,
        mesh=fine,
        in_specs=(
            P(ORIENT, SLAB),
            P(None, ORIENT, SLAB),
            P(SLAB),
            P(None, ORIENT),
            P(SLAB, ORIENT, None, None),
            P(SLAB, ORIENT, None, None),
        ),
        out_specs=P(SLAB, ORIENT, None, None),
        check_vma=False,
    )
```

```python
import functools

import jax
import jax.numpy as jnp
from jax import lax
from jax.experimental import pallas as pl
from jax.experimental.pallas import tpu as pltpu
from jax.sharding import Mesh, PartitionSpec as P

PIECE = 128
NAMES = ("yh", "z", "x", "yl", "core")
SIZES = (2, 8, 4, 4, 2)
ORIENT = ("yh", "z")
SLAB = ("x", "yl", "core")
bf16 = jnp.bfloat16
f32 = jnp.float32


def swapped(value, axis):
    return lax.ppermute(value, axis, [(0, 1), (1, 0)])


def exchanged(value, axis):
    return lax.all_to_all(value, axis, 0, 0, tiled=True)


def shared(value, axis, count):
    return exchanged(jnp.broadcast_to(value[None], (count,) + value.shape), axis)


def turned(block, step, axis="z", count=8):
    return lax.ppermute(block, axis, [(i, (i + step) % count) for i in range(count)])


STEPS = (0, 1, -1, 2, -2, 3, -3, 4)


def ring_gathered(block, held_back):
    got = [block]
    up = down = block
    for step in range(1, 5):
        up = turned(up, 1)
        got.append(up)
        if step < 4:
            down = turned(down, -1)
            got.append(down)
        if step == 2:
            held_back = lax.optimization_barrier((up, down, held_back))[2]
    return got, held_back


def kernel_params():
    return pltpu.CompilerParams(vmem_limit_bytes=24 * 2**20)


def ring_score_kernel(core_ref, z_ref, *refs):
    blocks, (weighted_ref, penalty_ref, far_ref, near_ref, plane_ref) = refs[:-5], refs[-5:]
    rows = blocks[0].shape[0]
    for step, block_ref in zip(STEPS, blocks):
        owner = lax.rem(z_ref[0] + 8 - step, 8)
        plane_ref[pl.ds(pl.multiple_of(owner * rows, rows), rows), :] = block_ref[...]
    score_kernel(core_ref, plane_ref, weighted_ref, penalty_ref, far_ref, near_ref)


def ring_scored(core, z, blocks, weighted, penalty):
    rows, pixels = blocks[0].shape
    rows *= len(blocks)
    columns = weighted.shape[0]
    side = jax.ShapeDtypeStruct((rows // 2, columns), f32)
    whole = pl.BlockSpec(memory_space=pltpu.VMEM)
    one = pl.BlockSpec(memory_space=pltpu.SMEM)
    return pl.pallas_call(
        ring_score_kernel,
        out_shape=(side, side, jax.ShapeDtypeStruct((rows, pixels), bf16)),
        in_specs=[one, one] + [whole] * (len(blocks) + 2),
        out_specs=(whole, whole, whole),
        compiler_params=kernel_params(),
        cost_estimate=pl.CostEstimate(
            flops=2 * rows * pixels * columns,
            bytes_accessed=2 * pixels * (2 * rows + columns) + 4 * rows * columns,
            transcendentals=0,
        ),
    )(core, z, *blocks, weighted, penalty)


def score_kernel(core_ref, image_ref, weighted_ref, penalty_ref, far_ref, near_ref):
    side = far_ref.shape[0]
    core = core_ref[0]
    for out_ref, at in ((far_ref, 1 - core), (near_ref, core)):
        rows = image_ref[pl.ds(pl.multiple_of(at * side, side), side), :]
        out_ref[...] = (
            lax.dot_general(
                rows, weighted_ref[...], (((1,), (1,)), ((), ())), preferred_element_type=f32
            )
            + penalty_ref[...]
        )


def scored(core, stored, weighted, penalty):
    rows, pixels = stored.shape
    columns = weighted.shape[0]
    side = jax.ShapeDtypeStruct((rows // 2, columns), f32)
    whole = pl.BlockSpec(memory_space=pltpu.VMEM)
    return pl.pallas_call(
        score_kernel,
        out_shape=(side, side),
        in_specs=[pl.BlockSpec(memory_space=pltpu.SMEM), whole, whole, whole],
        out_specs=(whole, whole),
        compiler_params=kernel_params(),
        cost_estimate=pl.CostEstimate(
            flops=2 * rows * pixels * columns,
            bytes_accessed=2 * pixels * (rows + columns) + 4 * rows * columns,
            transcendentals=0,
        ),
    )(core, stored, weighted, penalty)


def spots(slot_ref, start, count):
    at = start + lax.broadcasted_iota(jnp.int32, (count, slot_ref.shape[1]), 0)
    return jnp.where(at == slot_ref[...], 1.0, 0.0).astype(bf16)


def slice_kernel(
    core_ref, mine_ref, twin_ref, other_ref, own_ref, slot_ref, pieces_ref, away_ref, turned_ref
):
    step = pl.program_id(0)
    columns, rows = turned_ref.shape
    part = rows // 4
    per_class = pieces_ref.shape[0] // 16
    classes = columns // per_class

    @pl.when(step == 0)
    def _():
        for plane in range(2):
            for core in range(2):
                mine = mine_ref[:, plane].reshape(part, columns)
                twin = twin_ref[:, plane].reshape(part, columns)
                block = jnp.where(core_ref[0] == core, mine.astype(f32), twin.astype(f32))
                at = (2 * plane + core) * part
                turned_ref[:, at : at + part] = block.T.astype(bf16)

    slices = jnp.dot(
        turned_ref[:, : 2 * part], other_ref[...], preferred_element_type=f32
    ) + jnp.dot(turned_ref[:, 2 * part :], own_ref[...], preferred_element_type=f32)
    slices = slices.astype(bf16)
    many = slices.shape[1] // PIECE
    for p in range(many):
        to = pl.ds(pl.multiple_of((step * many + p) * per_class, 16), per_class)
        for k in range(classes):
            pieces_ref[to, k * PIECE : (k + 1) * PIECE] = slices[
                k * per_class : (k + 1) * per_class, p * PIECE : (p + 1) * PIECE
            ]

    @pl.when(step == pl.num_programs(0) - 1)
    def _():
        count = away_ref.shape[0]
        away_ref[...] = jnp.dot(
            spots(slot_ref, 6 * count, count), pieces_ref[...], preferred_element_type=f32
        ).astype(bf16)


def sliced(core, mine, twin, other_plane, own_plane, slot, slots):
    columns = mine.shape[3]
    rows, pixels = other_plane.shape
    pieces = slot.shape[1]
    width = columns * pixels // pieces
    steps = 4
    wide = pixels // steps
    fixed = lambda rank: lambda i: (0,) * rank
    shard = pl.BlockSpec(mine.shape, fixed(4))
    band = pl.BlockSpec((rows, wide), lambda i: (0, i))
    return pl.pallas_call(
        slice_kernel,
        grid=(steps,),
        out_shape=(
            jax.ShapeDtypeStruct((pieces, width), bf16),
            jax.ShapeDtypeStruct((slots, width), bf16),
        ),
        in_specs=[
            pl.BlockSpec(memory_space=pltpu.SMEM),
            shard,
            shard,
            band,
            band,
            pl.BlockSpec(slot.shape, fixed(2)),
        ],
        out_specs=(
            pl.BlockSpec((pieces, width), fixed(2)),
            pl.BlockSpec((slots, width), fixed(2)),
        ),
        scratch_shapes=[pltpu.VMEM((columns, 2 * rows), bf16)],
        compiler_params=kernel_params(),
        cost_estimate=pl.CostEstimate(
            flops=4 * rows * pixels * columns + 2 * slots * pieces * width,
            bytes_accessed=4 * rows * pixels + 2 * width * (pieces + slots),
            transcendentals=0,
        ),
    )(core, mine, twin, other_plane, own_plane, slot)


def away_kernel(slot_ref, pieces_ref, away_ref):
    count = away_ref.shape[0] // 3
    for row, part in enumerate((1, 3, 0)):
        away_ref[row * count : (row + 1) * count, :] = jnp.dot(
            spots(slot_ref, (4 + part) * count, count),
            pieces_ref[...],
            preferred_element_type=f32,
        ).astype(bf16)


def near_kernel(part, row, slot_ref, pieces_ref, got_ref, sum_ref):
    count = sum_ref.shape[0]
    near = jnp.dot(
        spots(slot_ref, part * count, count), pieces_ref[...], preferred_element_type=f32
    )
    got = got_ref[row * count : (row + 1) * count, :].astype(f32)
    sum_ref[...] = (near + got).astype(sum_ref.dtype)


def whole_call(kernel, out, flops, *args):
    whole = pl.BlockSpec(memory_space=pltpu.VMEM)
    moved = sum(x.size * x.dtype.itemsize for x in args)
    return pl.pallas_call(
        kernel,
        out_shape=out,
        in_specs=[whole] * len(args),
        out_specs=whole,
        compiler_params=kernel_params(),
        cost_estimate=pl.CostEstimate(flops=flops, bytes_accessed=moved, transcendentals=0),
    )(*args)


def slots_summed(slot, cut, away, count):
    pieces, width = cut.shape
    flops = 2 * count * pieces * width
    far = swapped(away, "core")
    rest = jax.ShapeDtypeStruct((3 * count, width), bf16)
    rest = whole_call(away_kernel, rest, 3 * flops, slot, cut)

    def near(part, row, got, dtype=bf16):
        out = jax.ShapeDtypeStruct((count, width), dtype)
        return whole_call(functools.partial(near_kernel, part, row), out, flops, slot, cut, got)

    two = near(2, 0, far)
    rest = lax.optimization_barrier((two, rest))[1]
    two = turned(two, 2, "x", 4)
    rest = swapped(rest, "core")
    one = turned(near(1, 0, rest), 1, "x", 4)
    three = turned(near(3, 1, rest), 3, "x", 4)
    summed = near(0, 2, rest, f32)
    for got in (two, one, three):
        summed = summed + got.astype(f32)
    return summed.astype(bf16)


def local(images, projections, noise_weight, prior_score, routing, insert_kernel):
    classes, orient_local, pixels = projections.shape
    columns = classes * orient_local
    rows = images.shape[0]
    orients, slabs, half = 16, 32, 16
    plane_rows = rows * orients // 2
    share = plane_rows // slabs
    blocks = pixels // PIECE
    pieces = orient_local * blocks
    voxels = insert_kernel.shape[1] * orients
    core = lax.axis_index("core")
    upper = lax.axis_index("yh") == 0
    core_one = core.reshape(1)

    where = routing[0].transpose(1, 0, 2)
    owner = where[:, :, 0].reshape(1, pieces)
    voxel = where[:, :, 1].reshape(1, pieces)
    ahead = (owner // 8 + 4 - lax.axis_index("x")) % 4
    slot = ((((owner % 2) ^ core) * 4 + ahead) * 4 + owner // 2 % 4) * voxels + voxel

    other = swapped(images, "yh")
    ring, other = ring_gathered(images, other)
    other_plane = lax.all_gather(other, "z", axis=0).reshape(plane_rows, pixels)

    widened = projections.astype(f32)
    product = widened * noise_weight[None, None, :]
    weighted = product.astype(bf16).reshape(columns, pixels)
    penalty = (-0.5 * jnp.sum(widened * product, axis=2)).reshape(1, columns)
    prior = prior_score.reshape(columns)

    def summed_scores(far, near):
        summed = (near + swapped(far, "core")).reshape(half, share, columns)
        return jnp.sum(exchanged(summed, ("x", "yl")), axis=0) + prior[None, :]

    z_one = lax.axis_index("z").reshape(1)
    far, near, own_plane = ring_scored(core_one, z_one, ring, weighted, penalty)
    own_scores = summed_scores(far, near)
    other_scores = summed_scores(*scored(core_one, other_plane, weighted, penalty))
    scores = jnp.stack([other_scores, own_scores])
    peak = jnp.max(scores, axis=2)
    mass = jnp.sum(jnp.exp(scores - peak[:, :, None]), axis=2)
    stats = jnp.stack([peak, mass])
    stats = jnp.where(upper, stats[:, ::-1], stats)
    stats = shared(stats.reshape(2, 2 * share), ORIENT, orients)
    top = jnp.max(stats[:, 0], axis=0)
    total = top + jnp.log(jnp.sum(stats[:, 1] * jnp.exp(stats[:, 0] - top[None]), axis=0))
    total = total.reshape(2, share)
    total = jnp.where(upper, total[::-1], total)
    own_weights = jnp.exp(scores - total[:, :, None]).astype(bf16)
    mine = shared(own_weights, ("x", "yl"), half)
    twin = swapped(mine, "core")

    cut, away = sliced(core_one, mine, twin, other_plane, own_plane, slot, 4 * voxels)
    width = classes * PIECE
    summed = slots_summed(slot, cut, away, 4 * voxels)
    summed = exchanged(summed.reshape(4 * orients, voxels // orients, width), ("yl", "yh", "z"))
    own_blocks = jnp.sum(summed.astype(f32), axis=0)
    rounded = own_blocks.astype(bf16).reshape(own_blocks.shape[0], classes, PIECE)
    volume = jnp.einsum("vkc,vce->vke", rounded, insert_kernel[0], preferred_element_type=f32)
    return volume[None]


def solution(mesh):
    fine = Mesh(mesh.devices.reshape(SIZES), NAMES)
    return jax.shard_map(
        local,
        mesh=fine,
        in_specs=(
            P(ORIENT, SLAB),
            P(None, ORIENT, SLAB),
            P(SLAB),
            P(None, ORIENT),
            P(SLAB, ORIENT, None, None),
            P(SLAB, ORIENT, None, None),
        ),
        out_specs=P(SLAB, ORIENT, None, None),
        check_vma=False,
    )
```

```python
import functools

import jax
import jax.numpy as jnp
from jax import lax
from jax.experimental import pallas as pl
from jax.experimental.pallas import tpu as pltpu
from jax.sharding import Mesh, PartitionSpec as P

PIECE = 128
SLICE = 50
SCORE = 50
NAMES = ("yh", "z", "x", "yl", "core")
SIZES = (2, 8, 4, 4, 2)
ORIENT = ("yh", "z")
SLAB = ("x", "yl", "core")
bf16 = jnp.bfloat16
f32 = jnp.float32


def swapped(value, axis):
    return lax.ppermute(value, axis, [(0, 1), (1, 0)])


def exchanged(value, axis):
    return lax.all_to_all(value, axis, 0, 0, tiled=True)


def shared(value, axis, count):
    return exchanged(jnp.broadcast_to(value[None], (count,) + value.shape), axis)


def turned(block, step, axis="z", count=8):
    return lax.ppermute(block, axis, [(i, (i + step) % count) for i in range(count)])


STEPS = (0, 1, -1, 2, -2, 3, -3, 4)


def ring_gathered(block, held_back):
    got = [block]
    up = down = block
    for step in range(1, 5):
        up = turned(up, 1)
        got.append(up)
        if step < 4:
            down = turned(down, -1)
            got.append(down)
        if step == 2:
            held_back = lax.optimization_barrier((up, down, held_back))[2]
    return got, held_back


def kernel_params(mebibytes=24):
    return pltpu.CompilerParams(vmem_limit_bytes=mebibytes * 2**20)


def ring_score_kernel(core_ref, z_ref, *refs):
    blocks, (weighted_ref, penalty_ref, far_ref, near_ref, plane_ref) = refs[:-5], refs[-5:]
    rows = blocks[0].shape[0]
    for step, block_ref in zip(STEPS, blocks):
        owner = lax.rem(z_ref[0] + 8 - step, 8)
        plane_ref[pl.ds(pl.multiple_of(owner * rows, rows), rows), :] = block_ref[...]
    score_kernel(core_ref, plane_ref, weighted_ref, penalty_ref, far_ref, near_ref)


def ring_scored(core, z, blocks, weighted, penalty):
    rows, pixels = blocks[0].shape
    rows *= len(blocks)
    columns = weighted.shape[0]
    side = jax.ShapeDtypeStruct((rows // 2, columns), f32)
    whole = pl.BlockSpec(memory_space=pltpu.VMEM)
    one = pl.BlockSpec(memory_space=pltpu.SMEM)
    return pl.pallas_call(
        ring_score_kernel,
        out_shape=(side, side, jax.ShapeDtypeStruct((rows, pixels), bf16)),
        in_specs=[one, one] + [whole] * (len(blocks) + 2),
        out_specs=(whole, whole, whole),
        compiler_params=kernel_params(),
        cost_estimate=pl.CostEstimate(
            flops=2 * rows * pixels * columns,
            bytes_accessed=2 * pixels * (2 * rows + columns) + 4 * rows * columns,
            transcendentals=0,
        ),
    )(core, z, *blocks, weighted, penalty)


def score_kernel(core_ref, image_ref, weighted_ref, penalty_ref, far_ref, near_ref):
    side = far_ref.shape[0]
    core = core_ref[0]
    for out_ref, at in ((far_ref, 1 - core), (near_ref, core)):
        rows = image_ref[pl.ds(pl.multiple_of(at * side, side), side), :]
        out_ref[...] = (
            lax.dot_general(
                rows, weighted_ref[...], (((1,), (1,)), ((), ())), preferred_element_type=f32
            )
            + penalty_ref[...]
        )


def scored(core, stored, weighted, penalty):
    rows, pixels = stored.shape
    columns = weighted.shape[0]
    side = jax.ShapeDtypeStruct((rows // 2, columns), f32)
    whole = pl.BlockSpec(memory_space=pltpu.VMEM)
    return pl.pallas_call(
        score_kernel,
        out_shape=(side, side),
        in_specs=[pl.BlockSpec(memory_space=pltpu.SMEM), whole, whole, whole],
        out_specs=(whole, whole),
        compiler_params=kernel_params(SCORE),
        cost_estimate=pl.CostEstimate(
            flops=2 * rows * pixels * columns,
            bytes_accessed=2 * pixels * (rows + columns) + 4 * rows * columns,
            transcendentals=0,
        ),
    )(core, stored, weighted, penalty)


def spots(slot_ref, start, count):
    at = start + lax.broadcasted_iota(jnp.int32, (count, slot_ref.shape[1]), 0)
    return jnp.where(at == slot_ref[...], 1.0, 0.0).astype(bf16)


def slice_kernel(
    core_ref, mine_ref, twin_ref, other_ref, own_ref, slot_ref, pieces_ref, away_ref, turned_ref
):
    step = pl.program_id(0)
    columns, rows = turned_ref.shape
    part = rows // 4
    per_class = pieces_ref.shape[0] // 16
    classes = columns // per_class

    @pl.when(step == 0)
    def _():
        for plane in range(2):
            for core in range(2):
                mine = mine_ref[:, plane].reshape(part, columns)
                twin = twin_ref[:, plane].reshape(part, columns)
                block = jnp.where(core_ref[0] == core, mine.astype(f32), twin.astype(f32))
                at = (2 * plane + core) * part
                turned_ref[:, at : at + part] = block.T.astype(bf16)

    slices = jnp.dot(
        turned_ref[:, : 2 * part], other_ref[...], preferred_element_type=f32
    ) + jnp.dot(turned_ref[:, 2 * part :], own_ref[...], preferred_element_type=f32)
    slices = slices.astype(bf16)
    many = slices.shape[1] // PIECE
    for p in range(many):
        to = pl.ds(pl.multiple_of((step * many + p) * per_class, 16), per_class)
        for k in range(classes):
            pieces_ref[to, k * PIECE : (k + 1) * PIECE] = slices[
                k * per_class : (k + 1) * per_class, p * PIECE : (p + 1) * PIECE
            ]

    @pl.when(step == pl.num_programs(0) - 1)
    def _():
        count = away_ref.shape[0]
        away_ref[...] = jnp.dot(
            spots(slot_ref, 6 * count, count), pieces_ref[...], preferred_element_type=f32
        ).astype(bf16)


def sliced(core, mine, twin, other_plane, own_plane, slot, slots):
    columns = mine.shape[3]
    rows, pixels = other_plane.shape
    pieces = slot.shape[1]
    width = columns * pixels // pieces
    steps = 4
    wide = pixels // steps
    fixed = lambda rank: lambda i: (0,) * rank
    shard = pl.BlockSpec(mine.shape, fixed(4))
    band = pl.BlockSpec((rows, wide), lambda i: (0, i))
    return pl.pallas_call(
        slice_kernel,
        grid=(steps,),
        out_shape=(
            jax.ShapeDtypeStruct((pieces, width), bf16),
            jax.ShapeDtypeStruct((slots, width), bf16),
        ),
        in_specs=[
            pl.BlockSpec(memory_space=pltpu.SMEM),
            shard,
            shard,
            band,
            band,
            pl.BlockSpec(slot.shape, fixed(2)),
        ],
        out_specs=(
            pl.BlockSpec((pieces, width), fixed(2)),
            pl.BlockSpec((slots, width), fixed(2)),
        ),
        scratch_shapes=[pltpu.VMEM((columns, 2 * rows), bf16)],
        compiler_params=kernel_params(SLICE),
        cost_estimate=pl.CostEstimate(
            flops=4 * rows * pixels * columns + 2 * slots * pieces * width,
            bytes_accessed=4 * rows * pixels + 2 * width * (pieces + slots),
            transcendentals=0,
        ),
    )(core, mine, twin, other_plane, own_plane, slot)


def away_kernel(slot_ref, pieces_ref, away_ref):
    count = away_ref.shape[0] // 3
    for row, part in enumerate((1, 3, 0)):
        away_ref[row * count : (row + 1) * count, :] = jnp.dot(
            spots(slot_ref, (4 + part) * count, count),
            pieces_ref[...],
            preferred_element_type=f32,
        ).astype(bf16)


def near_kernel(part, row, slot_ref, pieces_ref, got_ref, sum_ref):
    count = sum_ref.shape[0]
    near = jnp.dot(
        spots(slot_ref, part * count, count), pieces_ref[...], preferred_element_type=f32
    )
    got = got_ref[row * count : (row + 1) * count, :].astype(f32)
    sum_ref[...] = (near + got).astype(sum_ref.dtype)


def whole_call(kernel, out, flops, *args):
    whole = pl.BlockSpec(memory_space=pltpu.VMEM)
    moved = sum(x.size * x.dtype.itemsize for x in args)
    return pl.pallas_call(
        kernel,
        out_shape=out,
        in_specs=[whole] * len(args),
        out_specs=whole,
        compiler_params=kernel_params(),
        cost_estimate=pl.CostEstimate(flops=flops, bytes_accessed=moved, transcendentals=0),
    )(*args)


def slots_summed(slot, cut, away, count):
    pieces, width = cut.shape
    flops = 2 * count * pieces * width
    far = swapped(away, "core")
    rest = jax.ShapeDtypeStruct((3 * count, width), bf16)
    rest = whole_call(away_kernel, rest, 3 * flops, slot, cut)

    def near(part, row, got, dtype=bf16):
        out = jax.ShapeDtypeStruct((count, width), dtype)
        return whole_call(functools.partial(near_kernel, part, row), out, flops, slot, cut, got)

    two = near(2, 0, far)
    rest = lax.optimization_barrier((two, rest))[1]
    two = turned(two, 2, "x", 4)
    rest = swapped(rest, "core")
    one = turned(near(1, 0, rest), 1, "x", 4)
    three = turned(near(3, 1, rest), 3, "x", 4)
    summed = near(0, 2, rest, f32)
    for got in (two, one, three):
        summed = summed + got.astype(f32)
    return summed.astype(bf16)


def local(images, projections, noise_weight, prior_score, routing, insert_kernel):
    classes, orient_local, pixels = projections.shape
    columns = classes * orient_local
    rows = images.shape[0]
    orients, slabs, half = 16, 32, 16
    plane_rows = rows * orients // 2
    share = plane_rows // slabs
    blocks = pixels // PIECE
    pieces = orient_local * blocks
    voxels = insert_kernel.shape[1] * orients
    core = lax.axis_index("core")
    upper = lax.axis_index("yh") == 0
    core_one = core.reshape(1)

    where = routing[0].transpose(1, 0, 2)
    owner = where[:, :, 0].reshape(1, pieces)
    voxel = where[:, :, 1].reshape(1, pieces)
    ahead = (owner // 8 + 4 - lax.axis_index("x")) % 4
    slot = ((((owner % 2) ^ core) * 4 + ahead) * 4 + owner // 2 % 4) * voxels + voxel

    other = swapped(images, "yh")
    ring, other = ring_gathered(images, other)
    other_plane = lax.all_gather(other, "z", axis=0).reshape(plane_rows, pixels)

    widened = projections.astype(f32)
    product = widened * noise_weight[None, None, :]
    weighted = product.astype(bf16).reshape(columns, pixels)
    penalty = (-0.5 * jnp.sum(widened * product, axis=2)).reshape(1, columns)
    prior = prior_score.reshape(columns)

    def summed_scores(far, near):
        summed = (near + swapped(far, "core")).reshape(half, share, columns)
        return jnp.sum(exchanged(summed, ("x", "yl")), axis=0) + prior[None, :]

    z_one = lax.axis_index("z").reshape(1)
    far, near, own_plane = ring_scored(core_one, z_one, ring, weighted, penalty)
    own_scores = summed_scores(far, near)
    other_scores = summed_scores(*scored(core_one, other_plane, weighted, penalty))
    scores = jnp.stack([other_scores, own_scores])
    peak = jnp.max(scores, axis=2)
    mass = jnp.sum(jnp.exp(scores - peak[:, :, None]), axis=2)
    stats = jnp.stack([peak, mass])
    stats = jnp.where(upper, stats[:, ::-1], stats)
    stats = shared(stats.reshape(2, 2 * share), ORIENT, orients)
    top = jnp.max(stats[:, 0], axis=0)
    total = top + jnp.log(jnp.sum(stats[:, 1] * jnp.exp(stats[:, 0] - top[None]), axis=0))
    total = total.reshape(2, share)
    total = jnp.where(upper, total[::-1], total)
    own_weights = jnp.exp(scores - total[:, :, None]).astype(bf16)
    mine = shared(own_weights, ("x", "yl"), half)
    twin = swapped(mine, "core")

    cut, away = sliced(core_one, mine, twin, other_plane, own_plane, slot, 4 * voxels)
    width = classes * PIECE
    summed = slots_summed(slot, cut, away, 4 * voxels)
    summed = exchanged(summed.reshape(4 * orients, voxels // orients, width), ("yl", "yh", "z"))
    own_blocks = jnp.sum(summed.astype(f32), axis=0)
    rounded = own_blocks.astype(bf16).reshape(own_blocks.shape[0], classes, PIECE)
    volume = jnp.einsum("vkc,vce->vke", rounded, insert_kernel[0], preferred_element_type=f32)
    return volume[None]


def solution(mesh):
    fine = Mesh(mesh.devices.reshape(SIZES), NAMES)
    return jax.shard_map(
        local,
        mesh=fine,
        in_specs=(
            P(ORIENT, SLAB),
            P(None, ORIENT, SLAB),
            P(SLAB),
            P(None, ORIENT),
            P(SLAB, ORIENT, None, None),
            P(SLAB, ORIENT, None, None),
        ),
        out_specs=P(SLAB, ORIENT, None, None),
        check_vma=False,
    )
```
